128 devices in a mesh: wide: 32 (over z, x, core), eight: 4 (over y).
Axes of the slice: x: 4, y: 4, z: 4, core: 2. Of those that a mesh axis runs over, the one named last changes fastest.
Arguments:
- start_vectors: bfloat16 [512, 96, 4096], P('wide', 'eight'), may hold values from -6 to 6
- conductance: float32 [512, 4096], P('wide'), may hold values from 1 to 100
- counts: int32 [512], P('wide'), may hold values from 1 to 96, as said below
- element_of: int32 [512, 8], P('wide'), may hold values from 0 to 511, as said below
- capacity: float32 [512, 512], P(('wide', 'eight')), may hold values from 0.25 to 4
- coarse_in: float32 [512, 96, 64], P(('wide', 'eight')), may hold values from -6 to 6
Outputs:
- galerkin: float32 [512, 768, 768], P(('wide', 'eight'))
- coarse_out: float32 [512, 96, 64], P(('wide', 'eight'))
The draws below stay inside these ranges and needn't reach their ends.
Inputs may be any that keep to these rules, and one draw needn't show every extreme that they name: `counts`: some neighbourhood keeps exactly 96 basis functions. For each octant o, element_of[:, o] names every element exactly once. Element e belongs to device e // 4 in the order of wide+eight, and the 16 neighbourhoods of each index of wide name, over all their octants, exactly 1 elements of each device.
All inputs are finite; a program needn't handle non-finite values.
Results may differ from the reference program's by a relative error of at most 0.0004.
Values sent between devices are 32-bit elements; how exact they have to be, the bound alone decides.
A program may use at most 192 MiB of HBM per device.

```python
import math
import jax
import jax.numpy as jnp
from jax import lax

SIDE = 16
SLOTS = 96
VECS = 64
PASSES = 6
NBH_DEV = 16
CELLS = 4096
ECELLS = 512
NBH = 512
ELEMS = 512
N_WIDE = 32
N_EIGHT = 4


def draw_counts(key, part):
    key_base = jax.random.fold_in(key, 3)
    first_key, second_key, third_key = jax.random.split(key_base, 3)
    first_draw = jax.random.randint(first_key, (NBH,), 1, SLOTS + 1)
    second_draw = jax.random.randint(second_key, (NBH,), 1, SLOTS + 1)
    fullest = jax.random.randint(third_key, (), 0, NBH)
    kept = jnp.minimum(first_draw, second_draw)
    kept = jnp.where(jnp.arange(NBH) == fullest, SLOTS, kept)
    return kept.astype(jnp.int32)


def incidence(key):
    devices = N_WIDE * N_EIGHT
    key_base = jax.random.fold_in(key, 11)
    shuffle_key, relabel_key, tie_key = jax.random.split(key_base, 3)
    wide_index = jnp.arange(N_WIDE, dtype=jnp.int32)[:, None, None]
    octant_index = jnp.arange(8, dtype=jnp.int32)[None, :, None]
    member_index = jnp.arange(NBH_DEV, dtype=jnp.int32)[None, None, :]
    base_dest = (member_index + NBH_DEV * octant_index + N_EIGHT * wide_index) % devices
    base_dest = jnp.broadcast_to(base_dest, (N_WIDE, 8, NBH_DEV))
    shuffle_keys = jax.random.split(shuffle_key, N_WIDE * 8)
    shuffles = jax.vmap(lambda one_key: jax.random.permutation(one_key, NBH_DEV))(shuffle_keys)
    shuffles = shuffles.reshape(N_WIDE, 8, NBH_DEV).astype(jnp.int32)
    base_dest = jnp.take_along_axis(base_dest, shuffles, axis=2)
    relabel = jax.random.permutation(relabel_key, devices).astype(jnp.int32)
    dest_dev = relabel[base_dest]
    dest_by_octant = jnp.transpose(dest_dev, (1, 0, 2)).reshape(8, N_WIDE * NBH_DEV)
    tie_keys = jax.random.split(tie_key, 8)
    tie_break = jax.vmap(lambda one_key: jax.random.permutation(one_key, N_WIDE * NBH_DEV))(tie_keys).astype(jnp.int32)
    score = dest_by_octant * (N_WIDE * NBH_DEV) + tie_break
    ordering = jnp.argsort(score, axis=1)
    element_ids = jnp.argsort(ordering, axis=1)
    return jnp.transpose(element_ids).astype(jnp.int32)


def draw_element_of(key, part):
    return incidence(key)


def steps_of(own_key, shape, cuts, smallest, high):
    def one(axis_at, blocks):
        steps = jax.random.uniform(jax.random.fold_in(jax.random.fold_in(own_key, 6), axis_at), (blocks,), jnp.float32, smallest / len(cuts), high / len(cuts))
        return jnp.repeat(jnp.exp(steps), shape[axis_at] // blocks).reshape((-1,) + (1,) * (len(shape) - axis_at - 1))

    factor_of = one(*cuts[0])
    for cut in cuts[1:]:
        factor_of = factor_of * one(*cut)
    return factor_of


def centred(stream_key, extent, width, reach, cuts=(), kind=jnp.bfloat16):
    array = jax.random.normal(stream_key, extent, jnp.float32) * width
    if len(cuts) > 0:
        array = steps_of(stream_key, extent, cuts, -0.22, 0.18) * array
    return jnp.clip(array, min=-reach, max=reach).astype(kind)


def setup_inputs(seed: int = 0) -> dict:
    arg_keys = jax.random.split(jax.random.key(seed), 7)
    return {
        "start_vectors": centred(arg_keys[0], (NBH, SLOTS, CELLS), 1.0, 6.0, ((0, 32), (1, 4))),
        "conductance": jnp.clip(jnp.exp(math.log(100.0) - 4.6051702 * jax.random.uniform(arg_keys[1], (NBH, CELLS), jnp.float32) ** steps_of(arg_keys[1], (NBH, CELLS), ((0, 32),), -0.2, 0.2)), 1.0, 100.0),
        "counts": draw_counts(jax.random.fold_in(arg_keys[6], 71), 0),
        "element_of": draw_element_of(jax.random.fold_in(arg_keys[6], 71), 0),
        "capacity": jnp.clip(jnp.exp(math.log(4.0) - 2.7725887 * jax.random.uniform(arg_keys[4], (ELEMS, ECELLS), jnp.float32) ** steps_of(arg_keys[4], (ELEMS, ECELLS), ((0, 128),), -0.2, 0.2)), 0.25, 4.0),
        "coarse_in": centred(arg_keys[5], (NBH, SLOTS, VECS), 1.0, 6.0, ((0, 128),), jnp.float32),
    }


def stencil_weights(conductance, edge_cells):
    cubic_cells = conductance.reshape(conductance.shape[:-1] + (edge_cells, edge_cells, edge_cells))
    leading = cubic_cells.ndim - 3
    padded = jnp.pad(cubic_cells, [(0, 0)] * leading + [(1, 1)] * 3, mode='edge')
    diagonal = jnp.zeros_like(cubic_cells)
    neighbour_links = []
    strides = (edge_cells * edge_cells, edge_cells, 1)
    for direction in range(3):
        position = lax.broadcasted_iota(jnp.int32, cubic_cells.shape, leading + direction)
        for toward in (-1, 1):
            starts = [0] * leading + [1, 1, 1]
            starts[leading + direction] = 1 + toward
            limits = [starts[dim_index] + cubic_cells.shape[dim_index] for dim_index in range(cubic_cells.ndim)]
            beside = lax.slice(padded, starts, limits)
            face_weight = 0.5 * (cubic_cells + beside)
            diagonal = diagonal + face_weight
            inside = (position + toward >= 0) & (position + toward < edge_cells)
            linked = jnp.where(inside, face_weight, jnp.zeros_like(face_weight))
            neighbour_links.append((toward * strides[direction], linked.reshape(conductance.shape)))
    return (diagonal.reshape(conductance.shape), neighbour_links)

def operate(field, diagonal, neighbour_links, plane_span):
    cell_total = field.shape[-1]
    padded = jnp.pad(field, [(0, 0)] * (field.ndim - 1) + [(plane_span, plane_span)])
    result = diagonal * field
    for offset, linked in neighbour_links:
        moved = lax.slice_in_dim(padded, plane_span + offset, plane_span + offset + cell_total, axis=field.ndim - 1)
        result = result - linked * moved
    return result

def hat_bump(edge_cells):
    half_side = edge_cells // 2
    along = (jnp.arange(edge_cells, dtype=jnp.float32) + 0.5) / half_side
    rising = jnp.minimum(along, 2.0 - along)
    return (rising[:, None, None] * rising[None, :, None] * rising[None, None, :]).reshape(-1)

def filtered_basis(start, conductance, live, edge_cells, sweeps):
    diagonal, neighbour_links = stencil_weights(conductance, edge_cells)
    upper_bound = 2.0 * lax.optimization_barrier(jnp.max(diagonal, axis=-1))
    centre = (0.5625 * upper_bound)[..., None, None]
    radius = (0.4375 * upper_bound)[..., None, None]
    diagonal = diagonal[..., None, :]
    neighbour_links = [(offset, linked[..., None, :]) for offset, linked in neighbour_links]
    plane_span = edge_cells * edge_cells
    previous = start
    current = (operate(previous, diagonal, neighbour_links, plane_span) - centre * previous) / radius
    for repeat in range(sweeps - 1):
        previous, current = (current, 2.0 * (operate(current, diagonal, neighbour_links, plane_span) - centre * current) / radius - previous)
    norm_scale = lax.rsqrt(lax.optimization_barrier(jnp.mean(current * current, axis=-1, keepdims=True)) + 1e-05)
    return current * norm_scale * hat_bump(edge_cells) * live[..., None]

def octant_pieces(basis, edge_cells):
    half_side = edge_cells // 2
    leading = basis.shape[:-1]
    rank_lead = len(leading)
    cubic = basis.reshape(leading + (2, half_side, 2, half_side, 2, half_side))
    axes_order = tuple(range(rank_lead - 1)) + (rank_lead, rank_lead + 2, rank_lead + 4, rank_lead - 1, rank_lead + 1, rank_lead + 3, rank_lead + 5)
    cubic = jnp.transpose(cubic, axes_order)
    return cubic.reshape(leading[:-1] + (8, leading[-1], half_side * half_side * half_side))

def reference(start_vectors, conductance, counts, element_of, capacity, coarse_in):
    slot_ids = jnp.arange(SLOTS, dtype=jnp.int32)

    def one_hood(packed):
        start, local_cond, count = packed
        live = (slot_ids < count).astype(jnp.float32)
        basis = filtered_basis(start.astype(jnp.float32), local_cond, live, SIDE, PASSES)
        return octant_pieces(basis, SIDE)
    pieces = lax.map(one_hood, (start_vectors, conductance, counts))
    octants = jnp.arange(8, dtype=jnp.int32)
    contributor = jnp.zeros((ELEMS, 8), jnp.int32).at[element_of, octants[None, :]].set(jnp.arange(NBH, dtype=jnp.int32)[:, None])

    def one_element(packed):
        hoods, weight = packed
        gathered = pieces[hoods, octants].reshape(8 * SLOTS, ECELLS)
        galerkin = jnp.dot(gathered * weight[None, :], gathered.T, precision=lax.Precision.HIGHEST) / ECELLS
        coarse_rows = coarse_in[hoods].reshape(8 * SLOTS, VECS)
        applied = jnp.dot(galerkin, coarse_rows, precision=lax.Precision.HIGHEST)
        return (galerkin, applied.reshape(8, SLOTS, VECS))
    galerkin, applied = lax.map(one_element, (contributor, capacity))
    coarse_out = jnp.zeros((NBH, SLOTS, VECS), jnp.float32).at[contributor].add(applied)
    return (galerkin, coarse_out)
```

```python
import functools

import jax
import jax.numpy as jnp
from jax import lax
from jax.experimental import pallas as pl
from jax.experimental.pallas import tpu as pltpu
from jax.sharding import PartitionSpec as P

SIDE = 16
PLANE = SIDE * SIDE
CELLS = SIDE * PLANE
ECELLS = 512
ROWS = 8
LANES = 128
FRONT = 8
FIELD = FRONT + CELLS + PLANE + 8
GROUP = 4
BOTH = ("wide", "eight")


def rows_of(a, extra=0, count=SIDE):
    return pl.ds(FRONT + a * PLANE + extra, count)


def clear_ends(field):
    field[pl.ds(0, FRONT)] = jnp.zeros((FRONT, LANES), jnp.float32)
    field[pl.ds(FRONT + CELLS, PLANE + 8)] = jnp.zeros((PLANE + 8, LANES), jnp.float32)


def link_weights(cond, coef, field):
    hoods = cond.shape[0]
    clear_ends(field)

    def bring(a, carry):
        plane = cond[:, pl.ds(pl.multiple_of(a * PLANE, PLANE), PLANE)]
        wide = jnp.broadcast_to(plane[:, None, :], (hoods, ROWS, PLANE)).reshape(LANES, PLANE)
        field[rows_of(a, 0, PLANE)] = wide.T
        return carry

    lax.fori_loop(0, SIDE, bring, 0)
    spot = lax.broadcasted_iota(jnp.int32, (SIDE, LANES), 0)
    ends = ((spot == 0) | (spot == SIDE - 1)).astype(jnp.float32)

    def one(a, largest):
        ahead = jnp.where(a < SIDE - 1, 0.5, 0.0)
        behind = jnp.where(a > 0, 0.5, 0.0)
        rim = 2.0 - 2.0 * (ahead + behind)
        last_b = None
        for b in range(SIDE):
            own = field[rows_of(a, b * SIDE)]
            link_a = ahead * (own + field[rows_of(a, b * SIDE + PLANE)])
            past = jnp.maximum(a - 1, 0)
            past_a = behind * (own + field[rows_of(past, b * SIDE)])
            edge = own * (ends + (rim + (1.0 if b in (0, SIDE - 1) else 0.0)))
            next_c = jnp.where(spot < SIDE - 1, 0.5 * (own + field[rows_of(a, b * SIDE + 1)]), 0.0)
            last_c = jnp.where(spot > 0, 0.5 * (own + field[rows_of(a, b * SIDE - 1)]), 0.0)
            edge += next_c + last_c
            diagonal = edge + link_a + past_a
            if b < SIDE - 1:
                link_b = 0.5 * (own + field[rows_of(a, b * SIDE + SIDE)])
                coef[1, pl.ds(a * PLANE + b * SIDE, SIDE)] = link_b
                diagonal += link_b
            if last_b is not None:
                diagonal += last_b
            last_b = link_b
            coef[0, pl.ds(a * PLANE + b * SIDE, SIDE)] = link_a
            coef[2, pl.ds(a * PLANE + b * SIDE, SIDE)] = next_c
            coef[3, pl.ds(a * PLANE + b * SIDE, SIDE)] = last_c
            coef[4, pl.ds(a * PLANE + b * SIDE, SIDE)] = edge
            largest = jnp.maximum(largest, diagonal)
        return largest

    largest = lax.fori_loop(0, SIDE, one, jnp.zeros((SIDE, LANES), jnp.float32))
    radius = 0.4375 * 2.0 * jnp.max(largest, axis=0, keepdims=True)
    scale = jnp.broadcast_to(2.0 / radius, (SIDE, LANES))

    def fit(a, carry):
        for b in range(SIDE):
            at = pl.ds(a * PLANE + b * SIDE, SIDE)
            for k in range(5):
                if k == 1 and b == SIDE - 1:
                    continue
                value = coef[k, at] * scale
                coef[k, at] = value - 18.0 / 7.0 if k == 4 else value
        return carry

    lax.fori_loop(0, SIDE, fit, 0)


def sweep(coef, now, old, flux, first=False, squares=False):
    flux[...] = jnp.zeros_like(flux)

    def one(a, total):
        last_b = None
        here = now[rows_of(a)]
        for base in range(0, SIDE, GROUP):
            results = []
            for b in range(base, base + GROUP):
                at = pl.ds(a * PLANE + b * SIDE, SIDE)
                result = coef[4, at] * here + flux[pl.ds(b * SIDE, SIDE)]
                if last_b is not None:
                    result += last_b
                across = coef[0, at] * (now[rows_of(a, b * SIDE + PLANE)] - here)
                result -= across
                result -= coef[2, at] * now[rows_of(a, b * SIDE + 1)]
                result -= coef[3, at] * now[rows_of(a, b * SIDE - 1)]
                if b < SIDE - 1:
                    ahead = now[rows_of(a, b * SIDE + SIDE)]
                    last_b = coef[1, at] * (ahead - here)
                    result -= last_b
                    here = ahead
                result = 0.5 * result if first else result - old[rows_of(a, b * SIDE)]
                results.append((b, across, result))
            for b, across, result in results:
                flux[pl.ds(b * SIDE, SIDE)] = across
                old[rows_of(a, b * SIDE)] = result
                if squares:
                    total += result * result
        return total

    return lax.fori_loop(0, SIDE, one, jnp.zeros((SIDE, LANES), jnp.float32))


def filtered_chunk(chunk, start, coef, even, odd, flux):
    hoods, width = start.shape[:2]
    clear_ends(even)
    clear_ends(odd)

    def bring(a, carry):
        plane = start[:, :, pl.ds(pl.multiple_of(a * PLANE, PLANE), PLANE)].astype(jnp.float32)
        plane = plane[:, chunk * ROWS : (chunk + 1) * ROWS].reshape(LANES, PLANE)
        even[rows_of(a, 0, PLANE)] = plane.T
        return carry

    lax.fori_loop(0, SIDE, bring, 0)
    sweep(coef, even, odd, flux, first=True)

    def two(step, carry):
        sweep(coef, odd, even, flux)
        sweep(coef, even, odd, flux)
        return carry

    lax.fori_loop(0, 2, two, 0)
    total = sweep(coef, odd, even, flux, squares=True)
    return jnp.sum(total, axis=0, keepdims=True) * (1.0 / CELLS)


def hat(at):
    return min(at + 0.5, SIDE - 0.5 - at) / (SIDE // 2)


def octant_of(field, scale, octant):
    dx, dy, dz = octant // 4, octant // 2 % 2, octant % 2
    spot = lax.broadcasted_iota(jnp.int32, (8, LANES), 0).astype(jnp.float32) + 8.0 * dz
    scale = scale * (jnp.minimum(spot + 0.5, SIDE - 0.5 - spot) * (2.0 / SIDE))
    parts = []
    for a in range(8 * dx, 8 * dx + 8):
        for b in range(8 * dy, 8 * dy + 8):
            cells = field[pl.ds(FRONT + a * PLANE + b * SIDE + 8 * dz, 8)]
            parts.append(cells * (scale * (hat(a) * hat(b))))
    return jnp.concatenate(parts, axis=0).T


def filter_kernel(chunk, with_rows, dest, live, start, cond, *rest):
    if with_rows:
        rows, out, rows_out, coef, even, odd, flux = rest
    else:
        out, coef, even, odd, flux = rest
    hoods = start.shape[0]
    link_weights(cond, coef, even)
    mean = filtered_chunk(chunk, start, coef, even, odd, flux)
    scale = jnp.broadcast_to(lax.rsqrt(mean + 1e-05) * live[chunk : chunk + 1], (8, LANES))
    for octant in range(8):
        turned = octant_of(even, scale, octant)
        for n in range(hoods):
            out[dest[n * 8 + octant]] = turned[n * ROWS : (n + 1) * ROWS]
    if with_rows:
        for n in range(hoods):
            for octant in range(8):
                rows_out[dest[n * 8 + octant]] = rows[n]


def filtered(chunk, dest, live, start, cond, rows=None):
    hoods = start.shape[0]
    with_rows = rows is not None
    vmem = pl.BlockSpec(memory_space=pltpu.VMEM)
    out_shape = [jax.ShapeDtypeStruct((hoods * 8, ROWS, ECELLS), jnp.float32)]
    operands = [live, start, cond]
    if with_rows:
        out_shape.append(jax.ShapeDtypeStruct((hoods * 8,) + rows.shape[1:], jnp.float32))
        operands.append(rows)
    return pl.pallas_call(
        functools.partial(filter_kernel, chunk, with_rows),
        in_specs=[pl.BlockSpec(memory_space=pltpu.SMEM)] + [vmem] * len(operands),
        out_specs=[vmem] * len(out_shape),
        scratch_shapes=[
            pltpu.VMEM((5, CELLS, LANES), jnp.float32),
            pltpu.VMEM((FIELD, LANES), jnp.float32),
            pltpu.VMEM((FIELD, LANES), jnp.float32),
            pltpu.VMEM((PLANE, LANES), jnp.float32),
        ],
        out_shape=out_shape,
        compiler_params=pltpu.CompilerParams(vmem_limit_bytes=48 * 2**20),
        cost_estimate=pl.CostEstimate(
            flops=hoods * ROWS * CELLS * 120, bytes_accessed=6 * 2**20, transcendentals=0
        ),
        name="filter",
    )(dest, *operands)


def split(wide_value):
    high = wide_value.astype(jnp.bfloat16)
    return high, (wide_value - high.astype(jnp.float32)).astype(jnp.bfloat16)


def thrice(left, right, dims):
    dot = functools.partial(
        lax.dot_general, dimension_numbers=(dims, ((), ())), preferred_element_type=jnp.float32
    )
    (lh, ll), (rh, rl) = left, right
    return dot(lh, rh) + (dot(lh, rl) + dot(ll, rh))


def element_kernel(where, weight, *rest):
    pieces, rows = rest[:24], rest[24:32]
    out, back, high, low, vec_high, vec_low = rest[32:]
    element = pl.program_id(0)
    root = jnp.sqrt(weight[0]) * (1.0 / ECELLS) ** 0.5
    for o in range(8):
        parts = [pieces[o * 3 + ch][0, g] for g in range(4) for ch in range(3)]
        whole = jnp.concatenate(parts, axis=0) * root
        high[pl.ds(o * 96, 96)], low[pl.ds(o * 96, 96)] = split(whole)
        packed = rows[o][0]
        packed = jnp.concatenate([packed[g] for g in range(3)], axis=0)
        vec = jnp.concatenate([packed[:, :64], packed[:, 64:]], axis=0)
        vec_high[pl.ds(o * 96, 96)], vec_low[pl.ds(o * 96, 96)] = split(vec)

    def block(i):
        return pl.ds(i * 256, 256)

    for i in range(3):
        for j in range(i, 3):
            product = thrice(
                (high[block(i)], low[block(i)]), (high[block(j)], low[block(j)]), ((1,), (1,))
            )
            out[0, block(i), block(j)] = product
            if i != j:
                out[0, block(j), block(i)] = product.T
    vec = (vec_high[...], vec_low[...])
    for i in range(8):
        applied = thrice(split(out[0, pl.ds(i * 96, 96)]), vec, ((1,), (0,)))
        packed = jnp.concatenate([applied[:48], applied[48:]], axis=1)
        source = where[element * 8 + i]
        for g in range(3):
            back[source, g] = packed[g * 16 : (g + 1) * 16]
        back[source, 3] = jnp.zeros((16, LANES), jnp.float32)


def elements(where, weight, got, rows):
    count = weight.shape[0]
    sources = got[0].shape[0]

    def piece(o):
        return pl.BlockSpec((1, 4, ROWS, ECELLS), lambda e, where: (where[e * 8 + o], 0, 0, 0))

    def vecs(o):
        return pl.BlockSpec((1, 4, 16, LANES), lambda e, where: (where[e * 8 + o], 0, 0, 0))

    return pl.pallas_call(
        element_kernel,
        grid_spec=pltpu.PrefetchScalarGridSpec(
            num_scalar_prefetch=1,
            grid=(count,),
            in_specs=[pl.BlockSpec((1, 1, ECELLS), lambda e, where: (e, 0, 0))]
            + [piece(o) for o in range(8) for _ in range(3)]
            + [vecs(o) for o in range(8)],
            out_specs=[
                pl.BlockSpec((1, 768, 768), lambda e, where: (e, 0, 0)),
                pl.BlockSpec((sources, 4, 16, LANES), lambda e, where: (0, 0, 0, 0)),
            ],
            scratch_shapes=[
                pltpu.VMEM((768, ECELLS), jnp.bfloat16),
                pltpu.VMEM((768, ECELLS), jnp.bfloat16),
                pltpu.VMEM((768, 64), jnp.bfloat16),
                pltpu.VMEM((768, 64), jnp.bfloat16),
            ],
        ),
        out_shape=[
            jax.ShapeDtypeStruct((count, 768, 768), jnp.float32),
            jax.ShapeDtypeStruct((sources, 4, 16, LANES), jnp.float32),
        ],
        compiler_params=pltpu.CompilerParams(vmem_limit_bytes=48 * 2**20),
        name="elements",
    )(where, weight, *[got[ch] for _ in range(8) for ch in range(3)], *[rows] * 8)


def sum_kernel(dest, back, out):
    hoods = out.shape[0]
    for n in range(hoods):
        total = back[dest[n * 8]]
        for o in range(1, 8):
            total += back[dest[n * 8 + o]]
        out[n] = total


def summed(dest, back):
    hoods = dest.shape[0] // 8
    return pl.pallas_call(
        sum_kernel,
        in_specs=[pl.BlockSpec(memory_space=pltpu.SMEM), pl.BlockSpec(memory_space=pltpu.VMEM)],
        out_specs=pl.BlockSpec(memory_space=pltpu.VMEM),
        out_shape=jax.ShapeDtypeStruct((hoods,) + back.shape[1:], jnp.float32),
        name="sums",
    )(dest, back)


def body(start_vectors, conductance, counts, element_of, capacity, coarse_in):
    me = lax.axis_index("wide") * 4 + lax.axis_index("eight")
    group = lax.axis_index("eight")
    hoods = start_vectors.shape[0]
    count = capacity.shape[0]
    dest = (element_of // count).reshape(-1)
    everyone = lax.all_gather(element_of, "wide")
    names = me * count + jnp.arange(count, dtype=jnp.int32)
    hits = everyone[None] == names[:, None, None, None]
    indices = jnp.arange(everyone.shape[0], dtype=jnp.int32)[None, :, None, None]
    where = jnp.sum(jnp.where(hits, indices, 0), axis=(1, 2)).reshape(-1)

    packed = jnp.concatenate([coarse_in[:, :48], coarse_in[:, 48:]], axis=2)
    packed = lax.all_gather(packed, "eight", tiled=True)
    rows = lax.dynamic_slice_in_dim(packed, jnp.minimum(group, 2) * 16, 16, axis=1)

    slots = group * 24 + jnp.arange(24, dtype=jnp.int32).reshape(3, 1, ROWS)
    live = (slots < counts[None, :, None]).astype(jnp.float32).reshape(3, LANES)
    send = functools.partial(lax.all_to_all, axis_name=BOTH, split_axis=0, concat_axis=0, tiled=True)
    got = []
    rows_out = None
    for chunk in range(3):
        out = filtered(
            chunk, dest, live, start_vectors, conductance, rows if chunk == 2 else None
        )
        if chunk == 2:
            rows_out = out[1]
        got.append(send(out[0]).reshape(-1, 4, ROWS, ECELLS))
    got_rows = send(rows_out).reshape(-1, 4, 16, LANES)

    weight = capacity.reshape(count, 1, ECELLS)
    galerkin, back = elements(where, weight, got, got_rows)
    back = send(back.reshape(-1, 16, LANES))
    sums = summed(dest, back)
    mine = lax.all_to_all(sums, "eight", split_axis=0, concat_axis=0, tiled=True)
    mine = mine.reshape(4, hoods // 4, 16, LANES)[:3].transpose(1, 0, 2, 3).reshape(hoods // 4, 48, LANES)
    coarse_out = jnp.concatenate([mine[:, :, :64], mine[:, :, 64:]], axis=1)
    return (galerkin, coarse_out)


def solution(mesh):
    in_specs = (
        P("wide", "eight", None),
        P("wide", None),
        P("wide"),
        P("wide", None),
        P(BOTH, None),
        P(BOTH, None, None),
    )
    out_specs = (P(BOTH, None, None), P(BOTH, None, None))
    return jax.shard_map(body, mesh=mesh, in_specs=in_specs, out_specs=out_specs, check_vma=False)
```

```python
import functools

import jax
import jax.numpy as jnp
from jax import lax
from jax.experimental import pallas as pl
from jax.experimental.pallas import tpu as pltpu
from jax.sharding import PartitionSpec as P

SIDE = 16
PLANE = SIDE * SIDE
CELLS = SIDE * PLANE
ECELLS = 512
ROWS = 8
LANES = 128
FRONT = 8
FIELD = FRONT + CELLS + PLANE + 8
GROUP = 4
BOTH = ("wide", "eight")
MESH = pl.DeviceIdType.MESH


def rows_of(a, extra=0, count=SIDE):
    return pl.ds(FRONT + a * PLANE + extra, count)


def clear_ends(field):
    field[pl.ds(0, FRONT)] = jnp.zeros((FRONT, LANES), jnp.float32)
    field[pl.ds(FRONT + CELLS, PLANE + 8)] = jnp.zeros((PLANE + 8, LANES), jnp.float32)


def link_weights(cond, coef, field):
    hoods = cond.shape[0]
    clear_ends(field)

    def bring(a, carry):
        plane = cond[:, pl.ds(pl.multiple_of(a * PLANE, PLANE), PLANE)]
        wide = jnp.broadcast_to(plane[:, None, :], (hoods, ROWS, PLANE)).reshape(LANES, PLANE)
        field[rows_of(a, 0, PLANE)] = wide.T
        return carry

    lax.fori_loop(0, SIDE, bring, 0)
    spot = lax.broadcasted_iota(jnp.int32, (SIDE, LANES), 0)
    ends = ((spot == 0) | (spot == SIDE - 1)).astype(jnp.float32)

    def one(a, largest):
        ahead = jnp.where(a < SIDE - 1, 0.5, 0.0)
        behind = jnp.where(a > 0, 0.5, 0.0)
        rim = 2.0 - 2.0 * (ahead + behind)
        last_b = None
        for b in range(SIDE):
            own = field[rows_of(a, b * SIDE)]
            link_a = ahead * (own + field[rows_of(a, b * SIDE + PLANE)])
            past = jnp.maximum(a - 1, 0)
            past_a = behind * (own + field[rows_of(past, b * SIDE)])
            edge = own * (ends + (rim + (1.0 if b in (0, SIDE - 1) else 0.0)))
            next_c = jnp.where(spot < SIDE - 1, 0.5 * (own + field[rows_of(a, b * SIDE + 1)]), 0.0)
            last_c = jnp.where(spot > 0, 0.5 * (own + field[rows_of(a, b * SIDE - 1)]), 0.0)
            edge += next_c + last_c
            diagonal = edge + link_a + past_a
            if b < SIDE - 1:
                link_b = 0.5 * (own + field[rows_of(a, b * SIDE + SIDE)])
                coef[1, pl.ds(a * PLANE + b * SIDE, SIDE)] = link_b
                diagonal += link_b
            if last_b is not None:
                diagonal += last_b
            last_b = link_b
            coef[0, pl.ds(a * PLANE + b * SIDE, SIDE)] = link_a
            coef[2, pl.ds(a * PLANE + b * SIDE, SIDE)] = next_c
            coef[3, pl.ds(a * PLANE + b * SIDE, SIDE)] = last_c
            coef[4, pl.ds(a * PLANE + b * SIDE, SIDE)] = edge
            largest = jnp.maximum(largest, diagonal)
        return largest

    largest = lax.fori_loop(0, SIDE, one, jnp.zeros((SIDE, LANES), jnp.float32))
    radius = 0.4375 * 2.0 * jnp.max(largest, axis=0, keepdims=True)
    scale = jnp.broadcast_to(2.0 / radius, (SIDE, LANES))

    def fit(a, carry):
        for b in range(SIDE):
            at = pl.ds(a * PLANE + b * SIDE, SIDE)
            for k in range(5):
                if k == 1 and b == SIDE - 1:
                    continue
                value = coef[k, at] * scale
                coef[k, at] = value - 18.0 / 7.0 if k == 4 else value
        return carry

    lax.fori_loop(0, SIDE, fit, 0)


def sweep(coef, now, old, flux, first=False, squares=False):
    flux[...] = jnp.zeros_like(flux)

    def one(a, total):
        last_b = None
        here = now[rows_of(a)]
        for base in range(0, SIDE, GROUP):
            results = []
            for b in range(base, base + GROUP):
                at = pl.ds(a * PLANE + b * SIDE, SIDE)
                result = coef[4, at] * here + flux[pl.ds(b * SIDE, SIDE)]
                if last_b is not None:
                    result += last_b
                across = coef[0, at] * (now[rows_of(a, b * SIDE + PLANE)] - here)
                result -= across
                result -= coef[2, at] * now[rows_of(a, b * SIDE + 1)]
                result -= coef[3, at] * now[rows_of(a, b * SIDE - 1)]
                if b < SIDE - 1:
                    ahead = now[rows_of(a, b * SIDE + SIDE)]
                    last_b = coef[1, at] * (ahead - here)
                    result -= last_b
                    here = ahead
                result = 0.5 * result if first else result - old[rows_of(a, b * SIDE)]
                results.append((b, across, result))
            for b, across, result in results:
                flux[pl.ds(b * SIDE, SIDE)] = across
                old[rows_of(a, b * SIDE)] = result
                if squares:
                    total += result * result
        return total

    return lax.fori_loop(0, SIDE, one, jnp.zeros((SIDE, LANES), jnp.float32))


def filtered_chunk(chunk, start, coef, even, odd, flux):
    hoods, width = start.shape[:2]
    clear_ends(even)
    clear_ends(odd)

    def bring(a, carry):
        plane = start[:, :, pl.ds(pl.multiple_of(a * PLANE, PLANE), PLANE)].astype(jnp.float32)
        plane = plane[:, chunk * ROWS : (chunk + 1) * ROWS].reshape(LANES, PLANE)
        even[rows_of(a, 0, PLANE)] = plane.T
        return carry

    lax.fori_loop(0, SIDE, bring, 0)
    sweep(coef, even, odd, flux, first=True)

    def two(step, carry):
        sweep(coef, odd, even, flux)
        sweep(coef, even, odd, flux)
        return carry

    lax.fori_loop(0, 2, two, 0)
    total = sweep(coef, odd, even, flux, squares=True)
    return jnp.sum(total, axis=0, keepdims=True) * (1.0 / CELLS)


def hat(at):
    return min(at + 0.5, SIDE - 0.5 - at) / (SIDE // 2)


def octant_of(field, scale, octant):
    dx, dy, dz = octant // 4, octant // 2 % 2, octant % 2
    spot = lax.broadcasted_iota(jnp.int32, (8, LANES), 0).astype(jnp.float32) + 8.0 * dz
    scale = scale * (jnp.minimum(spot + 0.5, SIDE - 0.5 - spot) * (2.0 / SIDE))
    parts = []
    for a in range(8 * dx, 8 * dx + 8):
        for b in range(8 * dy, 8 * dy + 8):
            cells = field[pl.ds(FRONT + a * PLANE + b * SIDE + 8 * dz, 8)]
            parts.append(cells * (scale * (hat(a) * hat(b))))
    return jnp.concatenate(parts, axis=0).T


def partner(k, wide, eight):
    z, x, core = wide // 8, wide // 2 % 4, wide % 2
    z = (z + k // 16 + 2 * (k // 4) + 3 * k) % 4
    x = (x + k // 4 + k) % 4
    core = (core + k // 64 + k) % 2
    return (z * 4 + x) * 2 + core, (eight + k) % 4


def all_of(ref):
    return lambda sem: pltpu.make_async_copy(ref, ref, sem)


def exchange_kernel(
    order, live, start, cond, coarse, ids,
    got, got_rows, table,
    coef, even, odd, flux, pieces, outgoing, coarse_rows, outgoing_rows,
    send_sem, recv_sem, own_sem,
):
    wide, eight = lax.axis_index("wide"), lax.axis_index("eight")
    groups, wides = lax.axis_size("eight"), lax.axis_size("wide")
    devices = groups * wides
    me = wide * groups + eight
    hoods = start.shape[0]
    mine = coarse.shape[0]

    for n in range(mine):
        packed = jnp.concatenate([coarse[n, :48], coarse[n, 48:]], axis=1)
        coarse_rows[pl.ds(eight * mine + n, 1)] = packed[None]
    own_rows = coarse_rows.at[pl.ds(eight * mine, mine)]
    for k in range(1, groups):
        pltpu.make_async_remote_copy(
            src_ref=own_rows, dst_ref=own_rows, send_sem=send_sem.at[3], recv_sem=recv_sem.at[3],
            device_id=(wide, (eight + k) % groups), device_id_type=MESH,
        ).start()

    def tell(k, carry):
        pltpu.make_async_remote_copy(
            src_ref=ids, dst_ref=table.at[wide], send_sem=send_sem.at[4], recv_sem=recv_sem.at[4],
            device_id=((wide + k) % wides, eight), device_id_type=MESH,
        ).start()
        return carry

    lax.fori_loop(1, wides, tell, 0)
    own_ids = pltpu.make_async_copy(ids, table.at[wide], own_sem.at[4])
    own_ids.start()

    link_weights(cond, coef, even)

    three = coarse_rows.at[pl.ds(0, mine * (groups - 1))]
    all_of(three)(recv_sem.at[3]).wait()

    first = jnp.minimum(eight, 2) * 16

    def take_rows(to):
        outgoing_rows[pl.ds(to, 1)] = coarse_rows[pl.ds(order[to] // 8, 1), pl.ds(first, 16)]

    def send_rows(k, carry):
        to_wide, to_eight = partner(k, wide, eight)
        to = to_wide * groups + to_eight
        take_rows(to)
        pltpu.make_async_remote_copy(
            src_ref=outgoing_rows.at[to], dst_ref=got_rows.at[me], send_sem=send_sem.at[5],
            recv_sem=recv_sem.at[5], device_id=(to_wide, to_eight), device_id_type=MESH,
        ).start()
        return carry

    lax.fori_loop(1, devices, send_rows, 0)
    take_rows(me)
    kept_rows = pltpu.make_async_copy(outgoing_rows.at[me], got_rows.at[me], own_sem.at[5])
    kept_rows.start()
    kept = []
    for chunk in range(3):
        mean = filtered_chunk(chunk, start, coef, even, odd, flux)
        scale = jnp.broadcast_to(lax.rsqrt(mean + 1e-05) * live[chunk : chunk + 1], (8, LANES))
        for octant in range(8):
            turned = octant_of(even, scale, octant)
            for n in range(hoods):
                pieces[n * 8 + octant] = turned[n * ROWS : (n + 1) * ROWS]

        def send(k, carry):
            to_wide, to_eight = partner(k, wide, eight)
            to = to_wide * groups + to_eight
            outgoing[chunk, pl.ds(to, 1)] = pieces[pl.ds(order[to], 1)]
            pltpu.make_async_remote_copy(
                src_ref=outgoing.at[chunk, to], dst_ref=got.at[chunk, me], send_sem=send_sem.at[chunk],
                recv_sem=recv_sem.at[chunk], device_id=(to_wide, to_eight), device_id_type=MESH,
            ).start()
            return carry

        lax.fori_loop(1, devices, send, 0)
        outgoing[chunk, pl.ds(me, 1)] = pieces[pl.ds(order[me], 1)]
        kept.append(pltpu.make_async_copy(outgoing.at[chunk, me], got.at[chunk, me], own_sem.at[chunk]))
        kept[-1].start()

    own_ids.wait()
    kept_rows.wait()
    all_of(three)(send_sem.at[3]).wait()
    others = table.at[pl.ds(0, wides - 1)]
    all_of(others)(send_sem.at[4]).wait()
    all_of(others)(recv_sem.at[4]).wait()
    others = got_rows.at[pl.ds(0, devices - 1)]
    all_of(others)(send_sem.at[5]).wait()
    all_of(others)(recv_sem.at[5]).wait()
    for chunk in range(3):
        kept[chunk].wait()
        others = got.at[chunk, pl.ds(0, devices - 1)]
        all_of(others)(send_sem.at[chunk]).wait()
        all_of(others)(recv_sem.at[chunk]).wait()


def exchanged(order, live, start, cond, coarse, ids):
    hoods = start.shape[0]
    pieces = hoods * 8
    wides = lax.axis_size("wide")
    vmem = pl.BlockSpec(memory_space=pltpu.VMEM)
    hbm = pl.BlockSpec(memory_space=pl.ANY)
    f32 = jnp.float32
    return pl.pallas_call(
        exchange_kernel,
        in_specs=[pl.BlockSpec(memory_space=pltpu.SMEM)] + [vmem] * 5,
        out_specs=[hbm] * 3,
        out_shape=[
            jax.ShapeDtypeStruct((3, pieces, ROWS, ECELLS), f32),
            jax.ShapeDtypeStruct((pieces, 16, LANES), f32),
            jax.ShapeDtypeStruct((wides,) + ids.shape, jnp.int32),
        ],
        scratch_shapes=[
            pltpu.VMEM((5, CELLS, LANES), f32),
            pltpu.VMEM((FIELD, LANES), f32),
            pltpu.VMEM((FIELD, LANES), f32),
            pltpu.VMEM((PLANE, LANES), f32),
            pltpu.VMEM((pieces, ROWS, ECELLS), f32),
            pltpu.VMEM((3, pieces, ROWS, ECELLS), f32),
            pltpu.VMEM((hoods, 48, LANES), f32),
            pltpu.VMEM((pieces, 16, LANES), f32),
            pltpu.SemaphoreType.DMA((6,)),
            pltpu.SemaphoreType.DMA((6,)),
            pltpu.SemaphoreType.DMA((6,)),
        ],
        compiler_params=pltpu.CompilerParams(has_side_effects=True, vmem_limit_bytes=48 * 2**20),
        name="exchange",
    )(order, live, start, cond, coarse, ids)


def split(wide_value):
    high = wide_value.astype(jnp.bfloat16)
    return high, (wide_value - high.astype(jnp.float32)).astype(jnp.bfloat16)


def thrice(left, right, dims):
    dot = functools.partial(
        lax.dot_general, dimension_numbers=(dims, ((), ())), preferred_element_type=jnp.float32
    )
    (lh, ll), (rh, rl) = left, right
    return dot(lh, rh) + (dot(lh, rl) + dot(ll, rh))


def element_kernel(where, weight, *rest):
    pieces, rows = rest[:8], rest[8:16]
    out, back, high, low, vec_high, vec_low = rest[16:]
    element = pl.program_id(0)
    root = jnp.sqrt(weight[0]) * (1.0 / ECELLS) ** 0.5
    for o in range(8):
        parts = [pieces[o][ch, 0, g] for g in range(4) for ch in range(3)]
        whole = jnp.concatenate(parts, axis=0) * root
        high[pl.ds(o * 96, 96)], low[pl.ds(o * 96, 96)] = split(whole)
        packed = rows[o][0]
        packed = jnp.concatenate([packed[g] for g in range(3)], axis=0)
        vec = jnp.concatenate([packed[:, :64], packed[:, 64:]], axis=0)
        vec_high[pl.ds(o * 96, 96)], vec_low[pl.ds(o * 96, 96)] = split(vec)

    def block(i):
        return pl.ds(i * 256, 256)

    for i in range(3):
        for j in range(i, 3):
            product = thrice(
                (high[block(i)], low[block(i)]), (high[block(j)], low[block(j)]), ((1,), (1,))
            )
            out[0, block(i), block(j)] = product
            if i != j:
                out[0, block(j), block(i)] = product.T
    vec = (vec_high[...], vec_low[...])
    for i in range(8):
        applied = thrice(split(out[0, pl.ds(i * 96, 96)]), vec, ((1,), (0,)))
        packed = jnp.concatenate([applied[:48], applied[48:]], axis=1)
        source = where[element * 8 + i]
        for g in range(3):
            back[source, g] = packed[g * 16 : (g + 1) * 16]
        back[source, 3] = jnp.zeros((16, LANES), jnp.float32)


def elements(where, weight, got, rows):
    count = weight.shape[0]
    sources = got.shape[1]

    def piece(o):
        return pl.BlockSpec((3, 1, 4, ROWS, ECELLS), lambda e, where: (0, where[e * 8 + o], 0, 0, 0))

    def vecs(o):
        return pl.BlockSpec((1, 4, 16, LANES), lambda e, where: (where[e * 8 + o], 0, 0, 0))

    return pl.pallas_call(
        element_kernel,
        grid_spec=pltpu.PrefetchScalarGridSpec(
            num_scalar_prefetch=1,
            grid=(count,),
            in_specs=[pl.BlockSpec((1, 1, ECELLS), lambda e, where: (e, 0, 0))]
            + [piece(o) for o in range(8)]
            + [vecs(o) for o in range(8)],
            out_specs=[
                pl.BlockSpec((1, 768, 768), lambda e, where: (e, 0, 0)),
                pl.BlockSpec((sources, 4, 16, LANES), lambda e, where: (0, 0, 0, 0)),
            ],
            scratch_shapes=[
                pltpu.VMEM((768, ECELLS), jnp.bfloat16),
                pltpu.VMEM((768, ECELLS), jnp.bfloat16),
                pltpu.VMEM((768, 64), jnp.bfloat16),
                pltpu.VMEM((768, 64), jnp.bfloat16),
            ],
        ),
        out_shape=[
            jax.ShapeDtypeStruct((count, 768, 768), jnp.float32),
            jax.ShapeDtypeStruct((sources, 4, 16, LANES), jnp.float32),
        ],
        compiler_params=pltpu.CompilerParams(vmem_limit_bytes=48 * 2**20),
        name="elements",
    )(where, weight, *[got] * 8, *[rows] * 8)


def return_kernel(dest, back, out, returned, sums, send_sem, recv_sem, own_sem):
    wide, eight = lax.axis_index("wide"), lax.axis_index("eight")
    groups, wides = lax.axis_size("eight"), lax.axis_size("wide")
    devices = groups * wides
    me = wide * groups + eight
    mine = out.shape[1]

    def send(k, carry):
        to_wide, to_eight = partner(k, wide, eight)
        pltpu.make_async_remote_copy(
            src_ref=back.at[to_wide, to_eight], dst_ref=returned.at[me], send_sem=send_sem.at[0],
            recv_sem=recv_sem.at[0], device_id=(to_wide, to_eight), device_id_type=MESH,
        ).start()
        return carry

    lax.fori_loop(1, devices, send, 0)
    kept = pltpu.make_async_copy(back.at[wide, eight], returned.at[me], own_sem.at[0])
    kept.start()
    kept.wait()
    others = returned.at[pl.ds(0, devices - 1)]
    all_of(others)(recv_sem.at[0]).wait()
    for n in range(mine * groups):
        total = returned[dest[n * 8]]
        for o in range(1, 8):
            total += returned[dest[n * 8 + o]]
        sums[n] = total
    for k in range(1, groups):
        to = (eight + k) % groups
        pltpu.make_async_remote_copy(
            src_ref=sums.at[pl.ds(to * mine, mine)], dst_ref=out.at[eight], send_sem=send_sem.at[1],
            recv_sem=recv_sem.at[1], device_id=(wide, to), device_id_type=MESH,
        ).start()
    kept = pltpu.make_async_copy(sums.at[pl.ds(eight * mine, mine)], out.at[eight], own_sem.at[1])
    kept.start()
    kept.wait()
    three = out.at[pl.ds(0, groups - 1)]
    all_of(three)(recv_sem.at[1]).wait()
    all_of(three)(send_sem.at[1]).wait()
    all_of(others)(send_sem.at[0]).wait()


def returned_sums(dest, back):
    hoods = dest.shape[0] // 8
    groups = lax.axis_size("eight")
    devices = back.shape[0] * groups
    vmem = pl.BlockSpec(memory_space=pltpu.VMEM)
    return pl.pallas_call(
        return_kernel,
        in_specs=[pl.BlockSpec(memory_space=pltpu.SMEM), vmem],
        out_specs=vmem,
        out_shape=jax.ShapeDtypeStruct((groups, hoods // groups, 16, LANES), jnp.float32),
        scratch_shapes=[
            pltpu.VMEM((devices, 16, LANES), jnp.float32),
            pltpu.VMEM((hoods, 16, LANES), jnp.float32),
            pltpu.SemaphoreType.DMA((2,)),
            pltpu.SemaphoreType.DMA((2,)),
            pltpu.SemaphoreType.DMA((2,)),
        ],
        compiler_params=pltpu.CompilerParams(has_side_effects=True, vmem_limit_bytes=16 * 2**20),
        name="returns",
    )(dest, back)


def body(start_vectors, conductance, counts, element_of, capacity, coarse_in):
    eight = lax.axis_index("eight")
    me = lax.axis_index("wide") * lax.axis_size("eight") + eight
    hoods = start_vectors.shape[0]
    count = capacity.shape[0]
    dest = (element_of // count).reshape(-1)
    pieces = dest.shape[0]
    names = jnp.arange(pieces, dtype=jnp.int32)
    places = (element_of % count * 8 + jnp.arange(8, dtype=jnp.int32)[None, :]).reshape(-1)
    both = names * 1024 + places
    both = jnp.sum(jnp.where(dest[None, :] == names[:, None], both[None, :], 0), axis=1)
    order, ids = both // 1024, both % 1024
    slots = eight * 24 + jnp.arange(24, dtype=jnp.int32).reshape(3, 1, ROWS)
    live = (slots < counts[None, :, None]).astype(jnp.float32).reshape(3, LANES)
    got, got_rows, table = exchanged(
        order, live, start_vectors, conductance, coarse_in, jnp.broadcast_to(ids[None], (8, pieces))
    )
    wides = table.shape[0]
    came = lax.dynamic_slice_in_dim(table[:, 0], me, 1, axis=1)
    spots = jnp.arange(count * 8, dtype=jnp.int32)[None]
    sources = jnp.arange(wides, dtype=jnp.int32)[:, None]
    where = jnp.sum(jnp.where(came == spots, sources, 0), axis=0)
    galerkin, back = elements(
        where,
        capacity.reshape(count, 1, ECELLS),
        got.reshape(3, wides, 4, ROWS, ECELLS),
        got_rows.reshape(wides, 4, 16, LANES),
    )
    mine = returned_sums(dest, back)[:3].transpose(1, 0, 2, 3).reshape(hoods // 4, 48, LANES)
    coarse_out = jnp.concatenate([mine[:, :, :64], mine[:, :, 64:]], axis=1)
    return (galerkin, coarse_out)


def solution(mesh):
    in_specs = (
        P("wide", "eight", None),
        P("wide", None),
        P("wide"),
        P("wide", None),
        P(BOTH, None),
        P(BOTH, None, None),
    )
    out_specs = (P(BOTH, None, None), P(BOTH, None, None))
    return jax.shard_map(body, mesh=mesh, in_specs=in_specs, out_specs=out_specs, check_vma=False)
```

```python
import functools

import jax
import jax.numpy as jnp
from jax import lax
from jax.experimental import pallas as pl
from jax.experimental.pallas import tpu as pltpu
from jax.sharding import PartitionSpec as P

SIDE = 16
PLANE = SIDE * SIDE
CELLS = SIDE * PLANE
ECELLS = 512
ROWS = 8
LANES = 128
FRONT = 8
FIELD = FRONT + CELLS + PLANE + 8
GROUP = 4
BOTH = ("wide", "eight")
MESH = pl.DeviceIdType.MESH


def rows_of(a, extra=0, count=SIDE):
    return pl.ds(FRONT + a * PLANE + extra, count)


def clear_ends(field):
    field[pl.ds(0, FRONT)] = jnp.zeros((FRONT, LANES), jnp.float32)
    field[pl.ds(FRONT + CELLS, PLANE + 8)] = jnp.zeros((PLANE + 8, LANES), jnp.float32)


def link_weights(cond, coef, field):
    hoods = cond.shape[0]
    clear_ends(field)

    def bring(a, carry):
        plane = cond[:, pl.ds(pl.multiple_of(a * PLANE, PLANE), PLANE)]
        wide = jnp.broadcast_to(plane[:, None, :], (hoods, ROWS, PLANE)).reshape(LANES, PLANE)
        field[rows_of(a, 0, PLANE)] = wide.T
        return carry

    lax.fori_loop(0, SIDE, bring, 0)
    spot = lax.broadcasted_iota(jnp.int32, (SIDE, LANES), 0)
    ends = ((spot == 0) | (spot == SIDE - 1)).astype(jnp.float32)

    def one(a, largest):
        ahead = jnp.where(a < SIDE - 1, 0.5, 0.0)
        behind = jnp.where(a > 0, 0.5, 0.0)
        rim = 2.0 - 2.0 * (ahead + behind)
        last_b = None
        for b in range(SIDE):
            own = field[rows_of(a, b * SIDE)]
            link_a = ahead * (own + field[rows_of(a, b * SIDE + PLANE)])
            past = jnp.maximum(a - 1, 0)
            past_a = behind * (own + field[rows_of(past, b * SIDE)])
            edge = own * (ends + (rim + (1.0 if b in (0, SIDE - 1) else 0.0)))
            next_c = jnp.where(spot < SIDE - 1, 0.5 * (own + field[rows_of(a, b * SIDE + 1)]), 0.0)
            last_c = jnp.where(spot > 0, 0.5 * (own + field[rows_of(a, b * SIDE - 1)]), 0.0)
            edge += next_c + last_c
            diagonal = edge + link_a + past_a
            if b < SIDE - 1:
                link_b = 0.5 * (own + field[rows_of(a, b * SIDE + SIDE)])
                coef[1, pl.ds(a * PLANE + b * SIDE, SIDE)] = link_b
                diagonal += link_b
            if last_b is not None:
                diagonal += last_b
            last_b = link_b
            coef[0, pl.ds(a * PLANE + b * SIDE, SIDE)] = link_a
            coef[2, pl.ds(a * PLANE + b * SIDE, SIDE)] = next_c
            coef[3, pl.ds(a * PLANE + b * SIDE, SIDE)] = last_c
            coef[4, pl.ds(a * PLANE + b * SIDE, SIDE)] = edge
            largest = jnp.maximum(largest, diagonal)
        return largest

    largest = lax.fori_loop(0, SIDE, one, jnp.zeros((SIDE, LANES), jnp.float32))
    radius = 0.4375 * 2.0 * jnp.max(largest, axis=0, keepdims=True)
    scale = jnp.broadcast_to(2.0 / radius, (SIDE, LANES))

    def fit(a, carry):
        for b in range(SIDE):
            at = pl.ds(a * PLANE + b * SIDE, SIDE)
            for k in range(5):
                if k == 1 and b == SIDE - 1:
                    continue
                value = coef[k, at] * scale
                coef[k, at] = value - 18.0 / 7.0 if k == 4 else value
        return carry

    lax.fori_loop(0, SIDE, fit, 0)


def sweep(coef, now, old, flux, first=False, squares=False):
    flux[...] = jnp.zeros_like(flux)

    def one(a, total):
        last_b = None
        here = now[rows_of(a)]
        for base in range(0, SIDE, GROUP):
            results = []
            for b in range(base, base + GROUP):
                at = pl.ds(a * PLANE + b * SIDE, SIDE)
                result = coef[4, at] * here + flux[pl.ds(b * SIDE, SIDE)]
                if last_b is not None:
                    result += last_b
                across = coef[0, at] * (now[rows_of(a, b * SIDE + PLANE)] - here)
                result -= across
                result -= coef[2, at] * now[rows_of(a, b * SIDE + 1)]
                result -= coef[3, at] * now[rows_of(a, b * SIDE - 1)]
                if b < SIDE - 1:
                    ahead = now[rows_of(a, b * SIDE + SIDE)]
                    last_b = coef[1, at] * (ahead - here)
                    result -= last_b
                    here = ahead
                result = 0.5 * result if first else result - old[rows_of(a, b * SIDE)]
                results.append((b, across, result))
            for b, across, result in results:
                flux[pl.ds(b * SIDE, SIDE)] = across
                old[rows_of(a, b * SIDE)] = result
                if squares:
                    total += result * result
        return total

    return lax.fori_loop(0, SIDE, one, jnp.zeros((SIDE, LANES), jnp.float32))


def filtered_chunk(chunk, start, coef, even, odd, flux, meanwhile=None):
    hoods, width = start.shape[:2]
    clear_ends(even)
    clear_ends(odd)

    def bring(a, carry):
        plane = start[:, :, pl.ds(pl.multiple_of(a * PLANE, PLANE), PLANE)].astype(jnp.float32)
        plane = plane[:, chunk * ROWS : (chunk + 1) * ROWS].reshape(LANES, PLANE)
        even[rows_of(a, 0, PLANE)] = plane.T
        return carry

    lax.fori_loop(0, SIDE, bring, 0)
    sweep(coef, even, odd, flux, first=True)
    if meanwhile is not None:
        meanwhile()

    def two(step, carry):
        sweep(coef, odd, even, flux)
        sweep(coef, even, odd, flux)
        return carry

    lax.fori_loop(0, 2, two, 0)
    total = sweep(coef, odd, even, flux, squares=True)
    return jnp.sum(total, axis=0, keepdims=True) * (1.0 / CELLS)


def hat(at):
    return min(at + 0.5, SIDE - 0.5 - at) / (SIDE // 2)


def octant_of(field, scale, octant):
    dx, dy, dz = octant // 4, octant // 2 % 2, octant % 2
    spot = lax.broadcasted_iota(jnp.int32, (8, LANES), 0).astype(jnp.float32) + 8.0 * dz
    scale = scale * (jnp.minimum(spot + 0.5, SIDE - 0.5 - spot) * (2.0 / SIDE))
    parts = []
    for a in range(8 * dx, 8 * dx + 8):
        for b in range(8 * dy, 8 * dy + 8):
            cells = field[pl.ds(FRONT + a * PLANE + b * SIDE + 8 * dz, 8)]
            parts.append(cells * (scale * (hat(a) * hat(b))))
    return jnp.concatenate(parts, axis=0).T


def partner(k, wide, eight):
    z, x, core, four = wide >> 3, wide >> 1, wide, k >> 2
    z = (z + (k >> 4) + 2 * four + 3 * k) & 3
    x = (x + four + k) & 3
    core = (core + (k >> 6) + k) & 1
    return (z * 4 + x) * 2 + core, (eight + k) & 3


def greet(wide, eight):
    barrier = pltpu.get_barrier_semaphore()
    devices = lax.axis_size("wide") * lax.axis_size("eight")

    def one(k, carry):
        to = partner(k, wide, eight)
        pl.semaphore_signal(barrier, inc=1, device_id=to, device_id_type=MESH)
        return carry

    lax.fori_loop(1, devices, one, 0)
    return lambda: pl.semaphore_wait(barrier, devices - 1)


def all_of(ref):
    return lambda sem: pltpu.make_async_copy(ref, ref, sem)


def exchange_kernel(
    order, live, start, cond, coarse, ids,
    got, got_rows, table,
    coef, even, odd, flux, pieces, outgoing, coarse_rows, outgoing_rows,
    send_sem, recv_sem, own_sem,
):
    wide, eight = lax.axis_index("wide"), lax.axis_index("eight")
    groups, wides = lax.axis_size("eight"), lax.axis_size("wide")
    devices = groups * wides
    me = wide * groups + eight
    hoods = start.shape[0]
    mine = coarse.shape[0]

    all_here = greet(wide, eight)
    link_weights(cond, coef, even)
    for n in range(mine):
        packed = jnp.concatenate([coarse[n, :48], coarse[n, 48:]], axis=1)
        coarse_rows[pl.ds(eight * mine + n, 1)] = packed[None]
    all_here()
    own_rows = coarse_rows.at[pl.ds(eight * mine, mine)]
    for k in range(1, groups):
        pltpu.make_async_remote_copy(
            src_ref=own_rows, dst_ref=own_rows, send_sem=send_sem.at[3], recv_sem=recv_sem.at[3],
            device_id=(wide, (eight + k) % groups), device_id_type=MESH,
        ).start()

    def tell(k, carry):
        pltpu.make_async_remote_copy(
            src_ref=ids, dst_ref=table.at[wide], send_sem=send_sem.at[4], recv_sem=recv_sem.at[4],
            device_id=((wide + k) % wides, eight), device_id_type=MESH,
        ).start()
        return carry

    lax.fori_loop(1, wides, tell, 0)
    own_ids = pltpu.make_async_copy(ids, table.at[wide], own_sem.at[4])
    own_ids.start()

    three = coarse_rows.at[pl.ds(0, mine * (groups - 1))]
    first = jnp.minimum(eight, 2) * 16

    def take_rows(to):
        outgoing_rows[pl.ds(to, 1)] = coarse_rows[pl.ds(order[to] // 8, 1), pl.ds(first, 16)]

    def send_rows(k, carry):
        to_wide, to_eight = partner(k, wide, eight)
        to = to_wide * groups + to_eight
        take_rows(to)
        pltpu.make_async_remote_copy(
            src_ref=outgoing_rows.at[to], dst_ref=got_rows.at[me], send_sem=send_sem.at[5],
            recv_sem=recv_sem.at[5], device_id=(to_wide, to_eight), device_id_type=MESH,
        ).start()
        return carry

    kept_rows = pltpu.make_async_copy(outgoing_rows.at[me], got_rows.at[me], own_sem.at[5])

    def send_all_rows():
        all_of(three)(recv_sem.at[3]).wait()
        lax.fori_loop(1, devices, send_rows, 0)
        take_rows(me)
        kept_rows.start()

    kept = []
    for chunk in range(3):
        mean = filtered_chunk(
            chunk, start, coef, even, odd, flux, send_all_rows if chunk == 0 else None
        )
        scale = jnp.broadcast_to(lax.rsqrt(mean + 1e-05) * live[chunk : chunk + 1], (8, LANES))
        for octant in range(8):
            turned = octant_of(even, scale, octant)
            for n in range(hoods):
                pieces[n * 8 + octant] = turned[n * ROWS : (n + 1) * ROWS]

        def send(k, carry):
            to_wide, to_eight = partner(k, wide, eight)
            to = to_wide * groups + to_eight
            outgoing[chunk, pl.ds(to, 1)] = pieces[pl.ds(order[to], 1)]
            pltpu.make_async_remote_copy(
                src_ref=outgoing.at[chunk, to], dst_ref=got.at[chunk, me], send_sem=send_sem.at[chunk],
                recv_sem=recv_sem.at[chunk], device_id=(to_wide, to_eight), device_id_type=MESH,
            ).start()
            return carry

        lax.fori_loop(1, devices, send, 0)
        outgoing[chunk, pl.ds(me, 1)] = pieces[pl.ds(order[me], 1)]
        kept.append(pltpu.make_async_copy(outgoing.at[chunk, me], got.at[chunk, me], own_sem.at[chunk]))
        kept[-1].start()

    own_ids.wait()
    kept_rows.wait()
    all_of(three)(send_sem.at[3]).wait()
    others = table.at[pl.ds(0, wides - 1)]
    all_of(others)(send_sem.at[4]).wait()
    all_of(others)(recv_sem.at[4]).wait()
    others = got_rows.at[pl.ds(0, devices - 1)]
    all_of(others)(send_sem.at[5]).wait()
    all_of(others)(recv_sem.at[5]).wait()
    for chunk in range(3):
        kept[chunk].wait()
        others = got.at[chunk, pl.ds(0, devices - 1)]
        all_of(others)(send_sem.at[chunk]).wait()
        all_of(others)(recv_sem.at[chunk]).wait()


def exchanged(order, live, start, cond, coarse, ids):
    hoods = start.shape[0]
    pieces = hoods * 8
    wides = lax.axis_size("wide")
    vmem = pl.BlockSpec(memory_space=pltpu.VMEM)
    hbm = pl.BlockSpec(memory_space=pl.ANY)
    f32 = jnp.float32
    return pl.pallas_call(
        exchange_kernel,
        in_specs=[pl.BlockSpec(memory_space=pltpu.SMEM)] + [vmem] * 5,
        out_specs=[hbm] * 3,
        out_shape=[
            jax.ShapeDtypeStruct((3, pieces, ROWS, ECELLS), f32),
            jax.ShapeDtypeStruct((pieces, 16, LANES), f32),
            jax.ShapeDtypeStruct((wides,) + ids.shape, jnp.int32),
        ],
        scratch_shapes=[
            pltpu.VMEM((5, CELLS, LANES), f32),
            pltpu.VMEM((FIELD, LANES), f32),
            pltpu.VMEM((FIELD, LANES), f32),
            pltpu.VMEM((PLANE, LANES), f32),
            pltpu.VMEM((pieces, ROWS, ECELLS), f32),
            pltpu.VMEM((3, pieces, ROWS, ECELLS), f32),
            pltpu.VMEM((hoods, 48, LANES), f32),
            pltpu.VMEM((pieces, 16, LANES), f32),
            pltpu.SemaphoreType.DMA((6,)),
            pltpu.SemaphoreType.DMA((6,)),
            pltpu.SemaphoreType.DMA((6,)),
        ],
        compiler_params=pltpu.CompilerParams(
            collective_id=0, has_side_effects=True, vmem_limit_bytes=48 * 2**20),
        name="exchange",
    )(order, live, start, cond, coarse, ids)


def split(wide_value):
    high = wide_value.astype(jnp.bfloat16)
    return high, (wide_value - high.astype(jnp.float32)).astype(jnp.bfloat16)


def thrice(left, right, dims):
    dot = functools.partial(
        lax.dot_general, dimension_numbers=(dims, ((), ())), preferred_element_type=jnp.float32
    )
    (lh, ll), (rh, rl) = left, right
    return dot(lh, rh) + (dot(lh, rl) + dot(ll, rh))


def finish_kernel(
    where, places, dest, weight, pieces, rows,
    galerkin, out,
    high, low, applied, back, made, returned, sums, send_sem, recv_sem, own_sem, out_sem,
):
    wide, eight = lax.axis_index("wide"), lax.axis_index("eight")
    groups, wides = lax.axis_size("eight"), lax.axis_size("wide")
    devices = groups * wides
    me = wide * groups + eight
    mine = out.shape[1]
    count = weight.shape[0]
    all_here = greet(wide, eight)

    def apply(element, carry):
        root = jnp.sqrt(weight[element]) * (1.0 / ECELLS) ** 0.5
        vecs = []
        for o in range(8):
            source = where[element * 8 + o]
            parts = [pieces[ch, source, g] for g in range(4) for ch in range(3)]
            whole = jnp.concatenate(parts, axis=0) * root
            high[element, pl.ds(o * 96, 96)], low[element, pl.ds(o * 96, 96)] = split(whole)
            packed = jnp.concatenate([rows[source, g] for g in range(3)], axis=0)
            vecs += [packed[:, :64], packed[:, 64:]]
        vec = jnp.concatenate(vecs, axis=0).T
        whole = (high[element], low[element])
        seen = thrice(split(vec), whole, ((1,), (0,)))
        product = thrice(whole, split(seen), ((1,), (1,)))
        for o in range(8):
            halves = [product[o * 96 + h * 48 : o * 96 + h * 48 + 48] for h in range(2)]
            applied[element * 8 + o] = jnp.concatenate(halves, axis=1)
        return carry

    lax.fori_loop(0, count, apply, 0)

    def place(source, carry):
        packed = applied[places[source]]
        for g in range(3):
            back[source, g] = packed[g * 16 : g * 16 + 16]
        back[source, 3] = jnp.zeros((16, LANES), jnp.float32)
        return carry

    lax.fori_loop(0, wides, place, 0)
    all_here()

    def send(k, carry):
        to_wide, to_eight = partner(k, wide, eight)
        pltpu.make_async_remote_copy(
            src_ref=back.at[to_wide, to_eight], dst_ref=returned.at[me], send_sem=send_sem.at[0],
            recv_sem=recv_sem.at[0], device_id=(to_wide, to_eight), device_id_type=MESH,
        ).start()
        return carry

    lax.fori_loop(1, devices, send, 0)
    kept = pltpu.make_async_copy(back.at[wide, eight], returned.at[me], own_sem.at[0])
    kept.start()

    def matrix(element, carry):
        def block(i):
            return element, pl.ds(i * 256, 256)

        for i in range(3):
            for j in range(i, 3):
                product = thrice(
                    (high[block(i)], low[block(i)]), (high[block(j)], low[block(j)]), ((1,), (1,))
                )
                made[element, pl.ds(i * 256, 256), pl.ds(j * 256, 256)] = product
                if i != j:
                    made[element, pl.ds(j * 256, 256), pl.ds(i * 256, 256)] = product.T
        pltpu.make_async_copy(made.at[element], galerkin.at[element], out_sem.at[element]).start()
        return carry

    lax.fori_loop(0, count, matrix, 0)
    kept.wait()
    others = returned.at[pl.ds(0, devices - 1)]
    all_of(others)(recv_sem.at[0]).wait()

    def total_of(n, carry):
        total = returned[dest[n * 8]]
        for o in range(1, 8):
            total += returned[dest[n * 8 + o]]
        sums[n] = total
        return carry

    lax.fori_loop(0, mine * groups, total_of, 0)
    for k in range(1, groups):
        to = (eight + k) & 3
        pltpu.make_async_remote_copy(
            src_ref=sums.at[pl.ds(to * mine, mine)], dst_ref=out.at[eight], send_sem=send_sem.at[1],
            recv_sem=recv_sem.at[1], device_id=(wide, to), device_id_type=MESH,
        ).start()
    kept = pltpu.make_async_copy(sums.at[pl.ds(eight * mine, mine)], out.at[eight], own_sem.at[1])
    kept.start()
    kept.wait()
    three = out.at[pl.ds(0, groups - 1)]
    all_of(three)(recv_sem.at[1]).wait()
    all_of(three)(send_sem.at[1]).wait()
    all_of(others)(send_sem.at[0]).wait()
    for element in range(count):
        pltpu.make_async_copy(made.at[element], galerkin.at[element], out_sem.at[element]).wait()


def finished(where, places, dest, weight, got, rows):
    hoods = dest.shape[0] // 8
    count = weight.shape[0]
    groups = lax.axis_size("eight")
    wides = got.shape[1]
    devices = wides * groups
    smem, vmem = (pl.BlockSpec(memory_space=m) for m in (pltpu.SMEM, pltpu.VMEM))
    f32 = jnp.float32
    return pl.pallas_call(
        finish_kernel,
        in_specs=[smem] * 3 + [vmem] * 3,
        out_specs=[pl.BlockSpec(memory_space=pl.ANY), vmem],
        out_shape=[
            jax.ShapeDtypeStruct((count, 768, 768), f32),
            jax.ShapeDtypeStruct((groups, hoods // groups, 16, LANES), f32),
        ],
        scratch_shapes=[
            pltpu.VMEM((count, 768, ECELLS), jnp.bfloat16),
            pltpu.VMEM((count, 768, ECELLS), jnp.bfloat16),
            pltpu.VMEM((count * 8, 48, LANES), f32),
            pltpu.VMEM((wides, groups, 16, LANES), f32),
            pltpu.VMEM((count, 768, 768), f32),
            pltpu.VMEM((devices, 16, LANES), f32),
            pltpu.VMEM((hoods, 16, LANES), f32),
            pltpu.SemaphoreType.DMA((2,)),
            pltpu.SemaphoreType.DMA((2,)),
            pltpu.SemaphoreType.DMA((2,)),
            pltpu.SemaphoreType.DMA((count,)),
        ],
        compiler_params=pltpu.CompilerParams(
            collective_id=1, has_side_effects=True, vmem_limit_bytes=40 * 2**20
        ),
        name="finish",
    )(where, places, dest, weight, got, rows)


def body(start_vectors, conductance, counts, element_of, capacity, coarse_in):
    eight = lax.axis_index("eight")
    me = lax.axis_index("wide") * lax.axis_size("eight") + eight
    hoods = start_vectors.shape[0]
    count = capacity.shape[0]
    dest = (element_of // count).reshape(-1)
    pieces = dest.shape[0]
    names = jnp.arange(pieces, dtype=jnp.int32)
    places = (element_of % count * 8 + jnp.arange(8, dtype=jnp.int32)[None, :]).reshape(-1)
    both = names * 1024 + places
    both = jnp.sum(jnp.where(dest[None, :] == names[:, None], both[None, :], 0), axis=1)
    order, ids = both // 1024, both % 1024
    slots = eight * 24 + jnp.arange(24, dtype=jnp.int32).reshape(3, 1, ROWS)
    live = (slots < counts[None, :, None]).astype(jnp.float32).reshape(3, LANES)
    got, got_rows, table = exchanged(
        order, live, start_vectors, conductance, coarse_in, jnp.broadcast_to(ids[None], (8, pieces))
    )
    wides = table.shape[0]
    came = lax.dynamic_slice_in_dim(table[:, 0], me, 1, axis=1)
    spots = jnp.arange(count * 8, dtype=jnp.int32)[None]
    sources = jnp.arange(wides, dtype=jnp.int32)[:, None]
    where = jnp.sum(jnp.where(came == spots, sources, 0), axis=0)
    galerkin, mine = finished(
        where,
        came[:, 0],
        dest,
        capacity.reshape(count, 1, ECELLS),
        got.reshape(3, wides, 4, ROWS, ECELLS),
        got_rows.reshape(wides, 4, 16, LANES),
    )
    mine = mine[:3].transpose(1, 0, 2, 3).reshape(hoods // 4, 48, LANES)
    coarse_out = jnp.concatenate([mine[:, :, :64], mine[:, :, 64:]], axis=1)
    return (galerkin, coarse_out)


def solution(mesh):
    in_specs = (
        P("wide", "eight", None),
        P("wide", None),
        P("wide"),
        P("wide", None),
        P(BOTH, None),
        P(BOTH, None, None),
    )
    out_specs = (P(BOTH, None, None), P(BOTH, None, None))
    return jax.shard_map(body, mesh=mesh, in_specs=in_specs, out_specs=out_specs, check_vma=False)
```

```python
import functools

import jax
import jax.numpy as jnp
from jax import lax
from jax.experimental import pallas as pl
from jax.experimental.pallas import tpu as pltpu
from jax.sharding import PartitionSpec as P

SIDE = 16
PLANE = SIDE * SIDE
CELLS = SIDE * PLANE
ECELLS = 512
ROWS = 8
LANES = 128
FRONT = 8
FIELD = FRONT + CELLS + PLANE + 8
GROUP = 4
BOTH = ("wide", "eight")
MESH = pl.DeviceIdType.MESH


def rows_of(a, extra=0, count=SIDE):
    return pl.ds(FRONT + a * PLANE + extra, count)


def clear_ends(field):
    field[pl.ds(0, FRONT)] = jnp.zeros((FRONT, LANES), jnp.float32)
    field[pl.ds(FRONT + CELLS, PLANE + 8)] = jnp.zeros((PLANE + 8, LANES), jnp.float32)


def link_weights(cond, coef, field):
    hoods = cond.shape[0]
    clear_ends(field)

    def bring(a, carry):
        plane = cond[:, pl.ds(pl.multiple_of(a * PLANE, PLANE), PLANE)]
        wide = jnp.broadcast_to(plane[:, None, :], (hoods, ROWS, PLANE)).reshape(LANES, PLANE)
        field[rows_of(a, 0, PLANE)] = wide.T
        return carry

    lax.fori_loop(0, SIDE, bring, 0)
    spot = lax.broadcasted_iota(jnp.int32, (SIDE, LANES), 0)
    ends = ((spot == 0) | (spot == SIDE - 1)).astype(jnp.float32)

    def one(a, largest):
        ahead = jnp.where(a < SIDE - 1, 0.5, 0.0)
        behind = jnp.where(a > 0, 0.5, 0.0)
        rim = 2.0 - 2.0 * (ahead + behind)
        last_b = None
        for b in range(SIDE):
            own = field[rows_of(a, b * SIDE)]
            link_a = ahead * (own + field[rows_of(a, b * SIDE + PLANE)])
            past = jnp.maximum(a - 1, 0)
            past_a = behind * (own + field[rows_of(past, b * SIDE)])
            edge = own * (ends + (rim + (1.0 if b in (0, SIDE - 1) else 0.0)))
            next_c = jnp.where(spot < SIDE - 1, 0.5 * (own + field[rows_of(a, b * SIDE + 1)]), 0.0)
            last_c = jnp.where(spot > 0, 0.5 * (own + field[rows_of(a, b * SIDE - 1)]), 0.0)
            edge += next_c + last_c
            diagonal = edge + link_a + past_a
            if b < SIDE - 1:
                link_b = 0.5 * (own + field[rows_of(a, b * SIDE + SIDE)])
                coef[1, pl.ds(a * PLANE + b * SIDE, SIDE)] = link_b
                diagonal += link_b
            if last_b is not None:
                diagonal += last_b
            last_b = link_b
            coef[0, pl.ds(a * PLANE + b * SIDE, SIDE)] = link_a
            coef[2, pl.ds(a * PLANE + b * SIDE, SIDE)] = next_c
            coef[3, pl.ds(a * PLANE + b * SIDE, SIDE)] = last_c
            coef[4, pl.ds(a * PLANE + b * SIDE, SIDE)] = edge
            largest = jnp.maximum(largest, diagonal)
        return largest

    largest = lax.fori_loop(0, SIDE, one, jnp.zeros((SIDE, LANES), jnp.float32))
    radius = 0.4375 * 2.0 * jnp.max(largest, axis=0, keepdims=True)
    scale = jnp.broadcast_to(2.0 / radius, (SIDE, LANES))

    def fit(a, carry):
        for b in range(SIDE):
            at = pl.ds(a * PLANE + b * SIDE, SIDE)
            for k in range(5):
                if k == 1 and b == SIDE - 1:
                    continue
                value = coef[k, at] * scale
                coef[k, at] = value - 18.0 / 7.0 if k == 4 else value
        return carry

    lax.fori_loop(0, SIDE, fit, 0)


def sweep(coef, now, old, flux, first=False, squares=False):
    flux[...] = jnp.zeros_like(flux)

    def one(a, total):
        last_b = None
        here = now[rows_of(a)]
        for base in range(0, SIDE, GROUP):
            results = []
            for b in range(base, base + GROUP):
                at = pl.ds(a * PLANE + b * SIDE, SIDE)
                result = coef[4, at] * here + flux[pl.ds(b * SIDE, SIDE)]
                if last_b is not None:
                    result += last_b
                across = coef[0, at] * (now[rows_of(a, b * SIDE + PLANE)] - here)
                result -= across
                result -= coef[2, at] * now[rows_of(a, b * SIDE + 1)]
                result -= coef[3, at] * now[rows_of(a, b * SIDE - 1)]
                if b < SIDE - 1:
                    ahead = now[rows_of(a, b * SIDE + SIDE)]
                    last_b = coef[1, at] * (ahead - here)
                    result -= last_b
                    here = ahead
                result = 0.5 * result if first else result - old[rows_of(a, b * SIDE)]
                results.append((b, across, result))
            for b, across, result in results:
                flux[pl.ds(b * SIDE, SIDE)] = across
                old[rows_of(a, b * SIDE)] = result
                if squares:
                    total += result * result
        return total

    return lax.fori_loop(0, SIDE, one, jnp.zeros((SIDE, LANES), jnp.float32))


def filtered_chunk(chunk, start, coef, even, odd, flux, meanwhile=None):
    hoods, width = start.shape[:2]
    clear_ends(even)
    clear_ends(odd)

    def bring(a, carry):
        plane = start[:, :, pl.ds(pl.multiple_of(a * PLANE, PLANE), PLANE)].astype(jnp.float32)
        plane = plane[:, chunk * ROWS : (chunk + 1) * ROWS].reshape(LANES, PLANE)
        even[rows_of(a, 0, PLANE)] = plane.T
        return carry

    lax.fori_loop(0, SIDE, bring, 0)
    sweep(coef, even, odd, flux, first=True)
    if meanwhile is not None:
        meanwhile()

    def two(step, carry):
        sweep(coef, odd, even, flux)
        sweep(coef, even, odd, flux)
        return carry

    lax.fori_loop(0, 2, two, 0)
    total = sweep(coef, odd, even, flux, squares=True)
    return jnp.sum(total, axis=0, keepdims=True) * (1.0 / CELLS)


def hat(at):
    return min(at + 0.5, SIDE - 0.5 - at) / (SIDE // 2)


def octant_of(field, scale, octant):
    dx, dy, dz = octant // 4, octant // 2 % 2, octant % 2
    spot = lax.broadcasted_iota(jnp.int32, (8, LANES), 0).astype(jnp.float32) + 8.0 * dz
    scale = scale * (jnp.minimum(spot + 0.5, SIDE - 0.5 - spot) * (2.0 / SIDE))
    parts = []
    for a in range(8 * dx, 8 * dx + 8):
        for b in range(8 * dy, 8 * dy + 8):
            cells = field[pl.ds(FRONT + a * PLANE + b * SIDE + 8 * dz, 8)]
            parts.append(cells * (scale * (hat(a) * hat(b))))
    return jnp.concatenate(parts, axis=0).T


def partner(k, wide, eight):
    z, x, core, four = wide >> 3, wide >> 1, wide, k >> 2
    z = (z + (k >> 4) + 2 * four + 3 * k) & 3
    x = (x + four + k) & 3
    core = (core + (k >> 6) + k) & 1
    return (z * 4 + x) * 2 + core, (eight + k) & 3


def greet(wide, eight):
    barrier = pltpu.get_barrier_semaphore()
    devices = lax.axis_size("wide") * lax.axis_size("eight")

    def one(k, carry):
        to = partner(k, wide, eight)
        pl.semaphore_signal(barrier, inc=1, device_id=to, device_id_type=MESH)
        return carry

    lax.fori_loop(1, devices, one, 0)
    return lambda: pl.semaphore_wait(barrier, devices - 1)


def all_of(ref):
    return lambda sem: pltpu.make_async_copy(ref, ref, sem)


def exchange_kernel(
    order, live, start, cond, coarse, ids,
    got, got_rows, table,
    coef, even, odd, flux, pieces, outgoing, coarse_rows, outgoing_rows,
    send_sem, recv_sem, own_sem,
):
    wide, eight = lax.axis_index("wide"), lax.axis_index("eight")
    groups, wides = lax.axis_size("eight"), lax.axis_size("wide")
    devices = groups * wides
    me = wide * groups + eight
    hoods = start.shape[0]
    mine = coarse.shape[0]

    all_here = greet(wide, eight)
    link_weights(cond, coef, even)
    for n in range(mine):
        turned = coarse[n].T
        packed = jnp.concatenate([turned[:48], turned[48:]], axis=1)
        coarse_rows[pl.ds(eight * mine + n, 1)] = packed[None]
    all_here()
    own_rows = coarse_rows.at[pl.ds(eight * mine, mine)]
    for k in range(1, groups):
        pltpu.make_async_remote_copy(
            src_ref=own_rows, dst_ref=own_rows, send_sem=send_sem.at[3], recv_sem=recv_sem.at[3],
            device_id=(wide, (eight + k) % groups), device_id_type=MESH,
        ).start()

    def tell(k, carry):
        pltpu.make_async_remote_copy(
            src_ref=ids, dst_ref=table.at[wide], send_sem=send_sem.at[4], recv_sem=recv_sem.at[4],
            device_id=((wide + k) % wides, eight), device_id_type=MESH,
        ).start()
        return carry

    lax.fori_loop(1, wides, tell, 0)
    own_ids = pltpu.make_async_copy(ids, table.at[wide], own_sem.at[4])
    own_ids.start()

    three = coarse_rows.at[pl.ds(0, mine * (groups - 1))]
    first = jnp.minimum(eight, 2) * 16

    def take_rows(to):
        outgoing_rows[pl.ds(to, 1)] = coarse_rows[pl.ds(order[to] // 8, 1), pl.ds(first, 16)]

    def send_rows(k, carry):
        to_wide, to_eight = partner(k, wide, eight)
        to = to_wide * groups + to_eight
        take_rows(to)
        pltpu.make_async_remote_copy(
            src_ref=outgoing_rows.at[to], dst_ref=got_rows.at[me], send_sem=send_sem.at[5],
            recv_sem=recv_sem.at[5], device_id=(to_wide, to_eight), device_id_type=MESH,
        ).start()
        return carry

    kept_rows = pltpu.make_async_copy(outgoing_rows.at[me], got_rows.at[me], own_sem.at[5])

    def send_all_rows():
        all_of(three)(recv_sem.at[3]).wait()
        lax.fori_loop(1, devices, send_rows, 0)
        take_rows(me)
        kept_rows.start()

    kept = []
    for chunk in range(3):
        mean = filtered_chunk(
            chunk, start, coef, even, odd, flux, send_all_rows if chunk == 0 else None
        )
        scale = jnp.broadcast_to(lax.rsqrt(mean + 1e-05) * live[chunk : chunk + 1], (8, LANES))
        for octant in range(8):
            turned = octant_of(even, scale, octant)
            for n in range(hoods):
                pieces[n * 8 + octant] = turned[n * ROWS : (n + 1) * ROWS]

        def send(k, carry):
            to_wide, to_eight = partner(k, wide, eight)
            to = to_wide * groups + to_eight
            outgoing[chunk, pl.ds(to, 1)] = pieces[pl.ds(order[to], 1)]
            pltpu.make_async_remote_copy(
                src_ref=outgoing.at[chunk, to], dst_ref=got.at[chunk, me], send_sem=send_sem.at[chunk],
                recv_sem=recv_sem.at[chunk], device_id=(to_wide, to_eight), device_id_type=MESH,
            ).start()
            return carry

        lax.fori_loop(1, devices, send, 0)
        outgoing[chunk, pl.ds(me, 1)] = pieces[pl.ds(order[me], 1)]
        kept.append(pltpu.make_async_copy(outgoing.at[chunk, me], got.at[chunk, me], own_sem.at[chunk]))
        kept[-1].start()

    own_ids.wait()
    kept_rows.wait()
    all_of(three)(send_sem.at[3]).wait()
    others = table.at[pl.ds(0, wides - 1)]
    all_of(others)(send_sem.at[4]).wait()
    all_of(others)(recv_sem.at[4]).wait()
    others = got_rows.at[pl.ds(0, devices - 1)]
    all_of(others)(send_sem.at[5]).wait()
    all_of(others)(recv_sem.at[5]).wait()
    for chunk in range(3):
        kept[chunk].wait()
        others = got.at[chunk, pl.ds(0, devices - 1)]
        all_of(others)(send_sem.at[chunk]).wait()
        all_of(others)(recv_sem.at[chunk]).wait()


def exchanged(order, live, start, cond, coarse, ids):
    hoods = start.shape[0]
    pieces = hoods * 8
    wides = lax.axis_size("wide")
    vmem = pl.BlockSpec(memory_space=pltpu.VMEM)
    hbm = pl.BlockSpec(memory_space=pl.ANY)
    f32 = jnp.float32
    return pl.pallas_call(
        exchange_kernel,
        in_specs=[pl.BlockSpec(memory_space=pltpu.SMEM)] + [vmem] * 5,
        out_specs=[hbm] * 3,
        out_shape=[
            jax.ShapeDtypeStruct((3, pieces, ROWS, ECELLS), f32),
            jax.ShapeDtypeStruct((pieces, 16, LANES), f32),
            jax.ShapeDtypeStruct((wides,) + ids.shape, jnp.int32),
        ],
        scratch_shapes=[
            pltpu.VMEM((5, CELLS, LANES), f32),
            pltpu.VMEM((FIELD, LANES), f32),
            pltpu.VMEM((FIELD, LANES), f32),
            pltpu.VMEM((PLANE, LANES), f32),
            pltpu.VMEM((pieces, ROWS, ECELLS), f32),
            pltpu.VMEM((3, pieces, ROWS, ECELLS), f32),
            pltpu.VMEM((hoods, 48, LANES), f32),
            pltpu.VMEM((pieces, 16, LANES), f32),
            pltpu.SemaphoreType.DMA((6,)),
            pltpu.SemaphoreType.DMA((6,)),
            pltpu.SemaphoreType.DMA((6,)),
        ],
        compiler_params=pltpu.CompilerParams(
            collective_id=0, has_side_effects=True, vmem_limit_bytes=36 * 2**20),
        name="exchange",
    )(order, live, start, cond, coarse, ids)


def split(wide_value):
    high = wide_value.astype(jnp.bfloat16)
    return high, (wide_value - high.astype(jnp.float32)).astype(jnp.bfloat16)


def thrice(left, right, dims):
    dot = functools.partial(
        lax.dot_general, dimension_numbers=(dims, ((), ())), preferred_element_type=jnp.float32
    )
    (lh, ll), (rh, rl) = left, right
    return dot(lh, rh) + (dot(lh, rl) + dot(ll, rh))


def finish_kernel(
    where, places, dest, weight, pieces, rows,
    galerkin, out,
    high, low, applied, back, made, returned, sums, send_sem, recv_sem, own_sem, out_sem,
):
    wide, eight = lax.axis_index("wide"), lax.axis_index("eight")
    groups, wides = lax.axis_size("eight"), lax.axis_size("wide")
    devices = groups * wides
    me = wide * groups + eight
    mine = out.shape[1]
    count = weight.shape[0]
    all_here = greet(wide, eight)

    def apply(element, carry):
        root = jnp.sqrt(weight[pl.ds(element, 1)])
        vecs = []
        for o in range(8):
            source = where[element * 8 + o]
            parts = [pieces[ch, source, g] for g in range(4) for ch in range(3)]
            whole = jnp.concatenate(parts, axis=0) * root
            high[element, pl.ds(o * 96, 96)], low[element, pl.ds(o * 96, 96)] = split(whole)
            packed = jnp.concatenate([rows[source, g] for g in range(3)], axis=0)
            vecs += [packed[:, :64], packed[:, 64:]]
        vec = jnp.concatenate(vecs, axis=0).T
        whole = (high[element], low[element])
        seen = thrice(split(vec), whole, ((1,), (0,)))
        product = thrice(whole, split(seen * (1.0 / ECELLS)), ((1,), (1,)))
        for o in range(8):
            halves = [product[o * 96 + h * 48 : o * 96 + h * 48 + 48] for h in range(2)]
            applied[element * 8 + o] = jnp.concatenate(halves, axis=1)
        return carry

    lax.fori_loop(0, count, apply, 0)

    def place(source, carry):
        packed = applied[places[source]]
        for g in range(3):
            back[source, g] = packed[g * 16 : g * 16 + 16]
        back[source, 3] = jnp.zeros((16, LANES), jnp.float32)
        return carry

    lax.fori_loop(0, wides, place, 0)
    all_here()

    def send(k, carry):
        to_wide, to_eight = partner(k, wide, eight)
        pltpu.make_async_remote_copy(
            src_ref=back.at[to_wide, to_eight], dst_ref=returned.at[me], send_sem=send_sem.at[0],
            recv_sem=recv_sem.at[0], device_id=(to_wide, to_eight), device_id_type=MESH,
        ).start()
        return carry

    lax.fori_loop(1, devices, send, 0)
    kept = pltpu.make_async_copy(back.at[wide, eight], returned.at[me], own_sem.at[0])
    kept.start()

    def matrix(element, carry):
        def block(i):
            return element, pl.ds(i * 256, 256)

        for i in range(3):
            for j in range(i, 3):
                product = thrice(
                    (high[block(i)], low[block(i)]), (high[block(j)], low[block(j)]), ((1,), (1,))
                )
                made[element, pl.ds(i * 256, 256), pl.ds(j * 256, 256)] = product
                if i != j:
                    made[element, pl.ds(j * 256, 256), pl.ds(i * 256, 256)] = product.T
        pltpu.make_async_copy(made.at[element], galerkin.at[element], out_sem.at[element]).start()
        return carry

    lax.fori_loop(0, count, matrix, 0)
    kept.wait()
    others = returned.at[pl.ds(0, devices - 1)]
    all_of(others)(recv_sem.at[0]).wait()

    def total_of(n, carry):
        total = returned[dest[n * 8]]
        for o in range(1, 8):
            total += returned[dest[n * 8 + o]]
        sums[n] = total
        return carry

    lax.fori_loop(0, mine * groups, total_of, 0)
    for k in range(1, groups):
        to = (eight + k) & 3
        pltpu.make_async_remote_copy(
            src_ref=sums.at[pl.ds(to * mine, mine)], dst_ref=out.at[eight], send_sem=send_sem.at[1],
            recv_sem=recv_sem.at[1], device_id=(wide, to), device_id_type=MESH,
        ).start()
    kept = pltpu.make_async_copy(sums.at[pl.ds(eight * mine, mine)], out.at[eight], own_sem.at[1])
    kept.start()
    kept.wait()
    three = out.at[pl.ds(0, groups - 1)]
    all_of(three)(recv_sem.at[1]).wait()
    all_of(three)(send_sem.at[1]).wait()
    all_of(others)(send_sem.at[0]).wait()
    for element in range(count):
        pltpu.make_async_copy(made.at[element], galerkin.at[element], out_sem.at[element]).wait()


def finished(where, places, dest, weight, got, rows):
    hoods = dest.shape[0] // 8
    count = weight.shape[0]
    groups = lax.axis_size("eight")
    wides = got.shape[1]
    devices = wides * groups
    smem, vmem = (pl.BlockSpec(memory_space=m) for m in (pltpu.SMEM, pltpu.VMEM))
    f32 = jnp.float32
    return pl.pallas_call(
        finish_kernel,
        in_specs=[smem] * 3 + [vmem] * 3,
        out_specs=[pl.BlockSpec(memory_space=pl.ANY), vmem],
        out_shape=[
            jax.ShapeDtypeStruct((count, 768, 768), f32),
            jax.ShapeDtypeStruct((groups, hoods // groups, 16, LANES), f32),
        ],
        scratch_shapes=[
            pltpu.VMEM((count, 768, ECELLS), jnp.bfloat16),
            pltpu.VMEM((count, 768, ECELLS), jnp.bfloat16),
            pltpu.VMEM((count * 8, 48, LANES), f32),
            pltpu.VMEM((wides, groups, 16, LANES), f32),
            pltpu.VMEM((count, 768, 768), f32),
            pltpu.VMEM((devices, 16, LANES), f32),
            pltpu.VMEM((hoods, 16, LANES), f32),
            pltpu.SemaphoreType.DMA((2,)),
            pltpu.SemaphoreType.DMA((2,)),
            pltpu.SemaphoreType.DMA((2,)),
            pltpu.SemaphoreType.DMA((count,)),
        ],
        compiler_params=pltpu.CompilerParams(
            collective_id=1, has_side_effects=True, vmem_limit_bytes=28 * 2**20
        ),
        name="finish",
    )(where, places, dest, weight, got, rows)


def body(start_vectors, conductance, counts, element_of, capacity, coarse_in):
    eight = lax.axis_index("eight")
    me = lax.axis_index("wide") * lax.axis_size("eight") + eight
    hoods = start_vectors.shape[0]
    count = capacity.shape[0]
    dest = (element_of // count).reshape(-1)
    pieces = dest.shape[0]
    names = jnp.arange(pieces, dtype=jnp.int32)
    places = (element_of % count * 8 + jnp.arange(8, dtype=jnp.int32)[None, :]).reshape(-1)
    both = names * 1024 + places
    both = jnp.sum(jnp.where(dest[None, :] == names[:, None], both[None, :], 0), axis=1)
    order, ids = both // 1024, both % 1024
    slots = eight * 24 + jnp.arange(24, dtype=jnp.int32).reshape(3, 1, ROWS)
    live = (slots < counts[None, :, None]).astype(jnp.float32).reshape(3, LANES)
    got, got_rows, table = exchanged(
        order,
        live,
        start_vectors,
        conductance,
        coarse_in.transpose(0, 2, 1),
        jnp.broadcast_to(ids[None], (8, pieces)),
    )
    wides = table.shape[0]
    came = lax.dynamic_slice_in_dim(table[:, 0], me, 1, axis=1)
    spots = jnp.arange(count * 8, dtype=jnp.int32)[None]
    sources = jnp.arange(wides, dtype=jnp.int32)[:, None]
    where = jnp.sum(jnp.where(came == spots, sources, 0), axis=0)
    galerkin, mine = finished(
        where,
        came[:, 0],
        dest,
        capacity,
        got.reshape(3, wides, 4, ROWS, ECELLS),
        got_rows.reshape(wides, 4, 16, LANES),
    )
    galerkin = galerkin * (1.0 / ECELLS)
    mine = mine[:3].transpose(1, 0, 2, 3).reshape(hoods // 4, 48, LANES)
    coarse_out = jnp.concatenate([mine[:, :, :64], mine[:, :, 64:]], axis=1)
    return (galerkin, coarse_out)


def solution(mesh):
    in_specs = (
        P("wide", "eight", None),
        P("wide", None),
        P("wide"),
        P("wide", None),
        P(BOTH, None),
        P(BOTH, None, None),
    )
    out_specs = (P(BOTH, None, None), P(BOTH, None, None))
    return jax.shard_map(body, mesh=mesh, in_specs=in_specs, out_specs=out_specs, check_vma=False)
```

```python
import functools

import jax
import jax.numpy as jnp
from jax import lax
from jax.experimental import pallas as pl
from jax.experimental.pallas import tpu as pltpu
from jax.sharding import PartitionSpec as P

SIDE = 16
PLANE = SIDE * SIDE
CELLS = SIDE * PLANE
ECELLS = 512
ROWS = 8
LANES = 128
SHARE = 12
FRONT = 8
FIELD = FRONT + CELLS + PLANE + 8
GROUP = 4
BOTH = ("wide", "eight")
MESH = pl.DeviceIdType.MESH


def rows_of(a, extra=0, count=SIDE):
    return pl.ds(FRONT + a * PLANE + extra, count)


def clear_ends(field):
    field[pl.ds(0, FRONT)] = jnp.zeros((FRONT, LANES), jnp.float32)
    field[pl.ds(FRONT + CELLS, PLANE + 8)] = jnp.zeros((PLANE + 8, LANES), jnp.float32)


def bring_conductance(cond, field):
    hoods = cond.shape[0]
    clear_ends(field)

    def bring(a, carry):
        plane = cond[:, pl.ds(pl.multiple_of(a * PLANE, PLANE), PLANE)]
        wide = jnp.broadcast_to(plane[:, None, :], (hoods, ROWS, PLANE)).reshape(LANES, PLANE)
        field[rows_of(a, 0, PLANE)] = wide.T
        return carry

    lax.fori_loop(0, SIDE, bring, 0)


def link_weights(coef, field):
    spot = lax.broadcasted_iota(jnp.int32, (SIDE, LANES), 0)
    ends = ((spot == 0) | (spot == SIDE - 1)).astype(jnp.float32)

    def one(a, largest):
        ahead = jnp.where(a < SIDE - 1, 0.5, 0.0)
        behind = jnp.where(a > 0, 0.5, 0.0)
        rim = 2.0 - 2.0 * (ahead + behind)
        last_b = None
        for b in range(SIDE):
            own = field[rows_of(a, b * SIDE)]
            link_a = ahead * (own + field[rows_of(a, b * SIDE + PLANE)])
            past = jnp.maximum(a - 1, 0)
            past_a = behind * (own + field[rows_of(past, b * SIDE)])
            edge = own * (ends + (rim + (1.0 if b in (0, SIDE - 1) else 0.0)))
            next_c = jnp.where(spot < SIDE - 1, 0.5 * (own + field[rows_of(a, b * SIDE + 1)]), 0.0)
            last_c = jnp.where(spot > 0, 0.5 * (own + field[rows_of(a, b * SIDE - 1)]), 0.0)
            edge += next_c + last_c
            diagonal = edge + link_a + past_a
            if b < SIDE - 1:
                link_b = 0.5 * (own + field[rows_of(a, b * SIDE + SIDE)])
                coef[1, pl.ds(a * PLANE + b * SIDE, SIDE)] = link_b
                diagonal += link_b
            if last_b is not None:
                diagonal += last_b
            last_b = link_b
            coef[0, pl.ds(a * PLANE + b * SIDE, SIDE)] = link_a
            coef[2, pl.ds(a * PLANE + b * SIDE, SIDE)] = next_c
            coef[3, pl.ds(a * PLANE + b * SIDE, SIDE)] = last_c
            coef[4, pl.ds(a * PLANE + b * SIDE, SIDE)] = edge
            largest = jnp.maximum(largest, diagonal)
        return largest

    largest = lax.fori_loop(0, SIDE, one, jnp.zeros((SIDE, LANES), jnp.float32))
    radius = 0.4375 * 2.0 * jnp.max(largest, axis=0, keepdims=True)
    scale = jnp.broadcast_to(2.0 / radius, (SIDE, LANES))

    def fit(a, carry):
        for b in range(SIDE):
            at = pl.ds(a * PLANE + b * SIDE, SIDE)
            for k in range(5):
                if k == 1 and b == SIDE - 1:
                    continue
                value = coef[k, at] * scale
                coef[k, at] = value - 18.0 / 7.0 if k == 4 else value
        return carry

    lax.fori_loop(0, SIDE, fit, 0)


def sweep(coef, now, old, flux, first=False, squares=False):
    flux[...] = jnp.zeros_like(flux)

    def one(a, total):
        last_b = None
        here = now[rows_of(a)]
        for base in range(0, SIDE, GROUP):
            results = []
            for b in range(base, base + GROUP):
                at = pl.ds(a * PLANE + b * SIDE, SIDE)
                result = coef[4, at] * here + flux[pl.ds(b * SIDE, SIDE)]
                if last_b is not None:
                    result += last_b
                across = coef[0, at] * (now[rows_of(a, b * SIDE + PLANE)] - here)
                result -= across
                result -= coef[2, at] * now[rows_of(a, b * SIDE + 1)]
                result -= coef[3, at] * now[rows_of(a, b * SIDE - 1)]
                if b < SIDE - 1:
                    ahead = now[rows_of(a, b * SIDE + SIDE)]
                    last_b = coef[1, at] * (ahead - here)
                    result -= last_b
                    here = ahead
                result = 0.5 * result if first else result - old[rows_of(a, b * SIDE)]
                results.append((b, across, result))
            for b, across, result in results:
                flux[pl.ds(b * SIDE, SIDE)] = across
                old[rows_of(a, b * SIDE)] = result
                if squares:
                    total += result * result
        return total

    return lax.fori_loop(0, SIDE, one, jnp.zeros((SIDE, LANES), jnp.float32))


def filtered_chunk(chunk, start, coef, even, odd, flux, meanwhile=None):
    hoods, width = start.shape[:2]
    clear_ends(even)
    clear_ends(odd)

    def bring(a, carry):
        plane = start[:, :, pl.ds(pl.multiple_of(a * PLANE, PLANE), PLANE)].astype(jnp.float32)
        plane = plane[:, chunk * ROWS : (chunk + 1) * ROWS].reshape(LANES, PLANE)
        even[rows_of(a, 0, PLANE)] = plane.T
        return carry

    lax.fori_loop(0, SIDE, bring, 0)
    sweep(coef, even, odd, flux, first=True)
    if meanwhile is not None:
        meanwhile()

    def two(step, carry):
        sweep(coef, odd, even, flux)
        sweep(coef, even, odd, flux)
        return carry

    lax.fori_loop(0, 2, two, 0)
    total = sweep(coef, odd, even, flux, squares=True)
    return jnp.sum(total, axis=0, keepdims=True) * (1.0 / CELLS)


def hat(at):
    return min(at + 0.5, SIDE - 0.5 - at) / (SIDE // 2)


def octant_of(field, scale, octant):
    dx, dy, dz = octant // 4, octant // 2 % 2, octant % 2
    spot = lax.broadcasted_iota(jnp.int32, (8, LANES), 0).astype(jnp.float32) + 8.0 * dz
    scale = scale * (jnp.minimum(spot + 0.5, SIDE - 0.5 - spot) * (2.0 / SIDE))
    parts = []
    for a in range(8 * dx, 8 * dx + 8):
        for b in range(8 * dy, 8 * dy + 8):
            cells = field[pl.ds(FRONT + a * PLANE + b * SIDE + 8 * dz, 8)]
            parts.append(cells * (scale * (hat(a) * hat(b))))
    return jnp.concatenate(parts, axis=0).T


def partner(k, wide, eight):
    z, x, core, four = wide >> 3, wide >> 1, wide, k >> 2
    z = (z + (k >> 4) + 2 * four + 3 * k) & 3
    x = (x + four + k) & 3
    core = (core + (k >> 6) + k) & 1
    return (z * 4 + x) * 2 + core, (eight + k) & 3


def greet(wide, eight):
    barrier = pltpu.get_barrier_semaphore()
    devices = lax.axis_size("wide") * lax.axis_size("eight")

    def one(k, carry):
        to = partner(k, wide, eight)
        pl.semaphore_signal(barrier, inc=1, device_id=to, device_id_type=MESH)
        return carry

    lax.fori_loop(1, devices, one, 0)
    return lambda: pl.semaphore_wait(barrier, devices - 1)


def all_of(ref):
    return lambda sem: pltpu.make_async_copy(ref, ref, sem)


def exchange_kernel(
    order, counts, start, cond_hbm, coarse_hbm, ids,
    got, got_rows, table,
    coef, even, odd, flux, pieces, outgoing, coarse_rows, outgoing_rows, cond, coarse,
    send_sem, recv_sem, own_sem,
):
    wide, eight = lax.axis_index("wide"), lax.axis_index("eight")
    groups, wides = lax.axis_size("eight"), lax.axis_size("wide")
    devices = groups * wides
    me = wide * groups + eight
    hoods = start.shape[0]
    mine = coarse.shape[0]

    bring_cond = pltpu.make_async_copy(cond_hbm, cond, own_sem.at[6])
    bring_coarse = pltpu.make_async_copy(coarse_hbm, coarse, own_sem.at[7])
    bring_cond.start()
    bring_coarse.start()
    all_here = greet(wide, eight)
    lane = lax.broadcasted_iota(jnp.int32, (8, LANES), 1)
    limit = jnp.zeros((8, LANES), jnp.int32)
    for n in range(hoods):
        limit = jnp.where(lane // ROWS == n, counts[n], limit)
    limit -= eight * 24 + lane % ROWS
    bring_cond.wait()
    bring_coarse.wait()
    bring_conductance(cond, even)
    link_weights(coef, even)
    for n in range(mine):
        turned = coarse[n].T
        packed = jnp.concatenate([turned[:48], turned[48:]], axis=1)
        coarse_rows[pl.ds(eight * mine + n, 1)] = packed[None]
    all_here()
    own_rows = coarse_rows.at[pl.ds(eight * mine, mine)]
    for k in range(1, groups):
        pltpu.make_async_remote_copy(
            src_ref=own_rows, dst_ref=own_rows, send_sem=send_sem.at[3], recv_sem=recv_sem.at[3],
            device_id=(wide, (eight + k) % groups), device_id_type=MESH,
        ).start()

    def tell(k, carry):
        pltpu.make_async_remote_copy(
            src_ref=ids, dst_ref=table.at[wide], send_sem=send_sem.at[4], recv_sem=recv_sem.at[4],
            device_id=((wide + k) % wides, eight), device_id_type=MESH,
        ).start()
        return carry

    lax.fori_loop(1, wides, tell, 0)
    own_ids = pltpu.make_async_copy(ids, table.at[wide], own_sem.at[4])
    own_ids.start()

    three = coarse_rows.at[pl.ds(0, mine * (groups - 1))]
    first = eight * SHARE

    def take_rows(to):
        outgoing_rows[pl.ds(to, 1)] = coarse_rows[pl.ds(order[to] // 8, 1), pl.ds(first, SHARE)]

    def send_rows(k, carry):
        to_wide, to_eight = partner(k, wide, eight)
        to = to_wide * groups + to_eight
        take_rows(to)
        pltpu.make_async_remote_copy(
            src_ref=outgoing_rows.at[to], dst_ref=got_rows.at[me], send_sem=send_sem.at[5],
            recv_sem=recv_sem.at[5], device_id=(to_wide, to_eight), device_id_type=MESH,
        ).start()
        return carry

    kept_rows = pltpu.make_async_copy(outgoing_rows.at[me], got_rows.at[me], own_sem.at[5])

    def send_all_rows():
        all_of(three)(recv_sem.at[3]).wait()
        lax.fori_loop(1, devices, send_rows, 0)
        take_rows(me)
        kept_rows.start()

    kept = []
    for chunk in range(3):
        mean = filtered_chunk(
            chunk, start, coef, even, odd, flux, send_all_rows if chunk == 0 else None
        )
        live = (limit > chunk * ROWS).astype(jnp.float32)
        scale = jnp.broadcast_to(lax.rsqrt(mean + 1e-05), (8, LANES)) * live
        for octant in range(8):
            turned = octant_of(even, scale, octant)
            for n in range(hoods):
                pieces[n * 8 + octant] = turned[n * ROWS : (n + 1) * ROWS]

        def send(k, carry):
            to_wide, to_eight = partner(k, wide, eight)
            to = to_wide * groups + to_eight
            outgoing[chunk, pl.ds(to, 1)] = pieces[pl.ds(order[to], 1)]
            pltpu.make_async_remote_copy(
                src_ref=outgoing.at[chunk, to], dst_ref=got.at[chunk, me], send_sem=send_sem.at[chunk],
                recv_sem=recv_sem.at[chunk], device_id=(to_wide, to_eight), device_id_type=MESH,
            ).start()
            return carry

        lax.fori_loop(1, devices, send, 0)
        outgoing[chunk, pl.ds(me, 1)] = pieces[pl.ds(order[me], 1)]
        kept.append(pltpu.make_async_copy(outgoing.at[chunk, me], got.at[chunk, me], own_sem.at[chunk]))
        kept[-1].start()

    own_ids.wait()
    kept_rows.wait()
    all_of(three)(send_sem.at[3]).wait()
    others = table.at[pl.ds(0, wides - 1)]
    all_of(others)(send_sem.at[4]).wait()
    all_of(others)(recv_sem.at[4]).wait()
    others = got_rows.at[pl.ds(0, devices - 1)]
    all_of(others)(send_sem.at[5]).wait()
    all_of(others)(recv_sem.at[5]).wait()
    for chunk in range(3):
        kept[chunk].wait()
        others = got.at[chunk, pl.ds(0, devices - 1)]
        all_of(others)(send_sem.at[chunk]).wait()
        all_of(others)(recv_sem.at[chunk]).wait()


def exchanged(order, counts, start, cond, coarse, ids):
    hoods = start.shape[0]
    pieces = hoods * 8
    wides = lax.axis_size("wide")
    vmem = pl.BlockSpec(memory_space=pltpu.VMEM)
    hbm = pl.BlockSpec(memory_space=pl.ANY)
    f32 = jnp.float32
    return pl.pallas_call(
        exchange_kernel,
        in_specs=[pl.BlockSpec(memory_space=pltpu.SMEM)] * 2 + [vmem, hbm, hbm, vmem],
        out_specs=[hbm] * 3,
        out_shape=[
            jax.ShapeDtypeStruct((3, pieces, ROWS, ECELLS), f32),
            jax.ShapeDtypeStruct((pieces, SHARE, LANES), f32),
            jax.ShapeDtypeStruct((wides,) + ids.shape, jnp.int32),
        ],
        scratch_shapes=[
            pltpu.VMEM((5, CELLS, LANES), f32),
            pltpu.VMEM((FIELD, LANES), f32),
            pltpu.VMEM((FIELD, LANES), f32),
            pltpu.VMEM((PLANE, LANES), f32),
            pltpu.VMEM((pieces, ROWS, ECELLS), f32),
            pltpu.VMEM((3, pieces, ROWS, ECELLS), f32),
            pltpu.VMEM((hoods, 48, LANES), f32),
            pltpu.VMEM((pieces, SHARE, LANES), f32),
            pltpu.VMEM(cond.shape, f32),
            pltpu.VMEM(coarse.shape, f32),
            pltpu.SemaphoreType.DMA((6,)),
            pltpu.SemaphoreType.DMA((6,)),
            pltpu.SemaphoreType.DMA((8,)),
        ],
        compiler_params=pltpu.CompilerParams(
            collective_id=0, has_side_effects=True, vmem_limit_bytes=36 * 2**20),
        name="exchange",
    )(order, counts, start, cond, coarse, ids)


def split(wide_value):
    high = wide_value.astype(jnp.bfloat16)
    return high, (wide_value - high.astype(jnp.float32)).astype(jnp.bfloat16)


def thrice(left, right, dims):
    dot = functools.partial(
        lax.dot_general, dimension_numbers=(dims, ((), ())), preferred_element_type=jnp.float32
    )
    (lh, ll), (rh, rl) = left, right
    return dot(lh, rh) + (dot(lh, rl) + dot(ll, rh))


def finish_kernel(
    where, places, dest, weight, pieces, rows,
    galerkin, out,
    high, low, applied, back, made, returned, sums, send_sem, recv_sem, own_sem, out_sem,
):
    wide, eight = lax.axis_index("wide"), lax.axis_index("eight")
    groups, wides = lax.axis_size("eight"), lax.axis_size("wide")
    devices = groups * wides
    me = wide * groups + eight
    mine = out.shape[1]
    count = weight.shape[0]
    all_here = greet(wide, eight)

    def apply(element, carry):
        root = jnp.sqrt(weight[pl.ds(element, 1)])
        vecs = []
        for o in range(8):
            source = where[element * 8 + o]
            parts = [pieces[ch, source, g] for g in range(4) for ch in range(3)]
            whole = jnp.concatenate(parts, axis=0) * root
            high[element, pl.ds(o * 96, 96)], low[element, pl.ds(o * 96, 96)] = split(whole)
            packed = jnp.concatenate([rows[source, g] for g in range(4)], axis=0)
            vecs += [packed[:, :64], packed[:, 64:]]
        vec = jnp.concatenate(vecs, axis=0).T
        whole = (high[element], low[element])
        seen = thrice(split(vec), whole, ((1,), (0,)))
        product = thrice(whole, split(seen * (1.0 / ECELLS)), ((1,), (1,)))
        for o in range(8):
            halves = [product[o * 96 + h * 48 : o * 96 + h * 48 + 48] for h in range(2)]
            applied[element * 8 + o] = jnp.concatenate(halves, axis=1)
        return carry

    lax.fori_loop(0, count, apply, 0)

    def place(source, carry):
        packed = applied[places[source]]
        for g in range(4):
            back[source, g] = packed[g * SHARE : (g + 1) * SHARE]
        return carry

    lax.fori_loop(0, wides, place, 0)
    all_here()

    def send(k, carry):
        to_wide, to_eight = partner(k, wide, eight)
        pltpu.make_async_remote_copy(
            src_ref=back.at[to_wide, to_eight], dst_ref=returned.at[me], send_sem=send_sem.at[0],
            recv_sem=recv_sem.at[0], device_id=(to_wide, to_eight), device_id_type=MESH,
        ).start()
        return carry

    lax.fori_loop(1, devices, send, 0)
    kept = pltpu.make_async_copy(back.at[wide, eight], returned.at[me], own_sem.at[0])
    kept.start()

    def matrix(element, carry):
        def block(i):
            return element, pl.ds(i * 256, 256)

        for i in range(3):
            for j in range(i, 3):
                product = thrice(
                    (high[block(i)], low[block(i)]), (high[block(j)], low[block(j)]), ((1,), (1,))
                )
                made[element, pl.ds(i * 256, 256), pl.ds(j * 256, 256)] = product
                if i != j:
                    made[element, pl.ds(j * 256, 256), pl.ds(i * 256, 256)] = product.T
        pltpu.make_async_copy(made.at[element], galerkin.at[element], out_sem.at[element]).start()
        return carry

    lax.fori_loop(0, count, matrix, 0)
    kept.wait()
    others = returned.at[pl.ds(0, devices - 1)]
    all_of(others)(recv_sem.at[0]).wait()

    def total_of(n, carry):
        total = returned[dest[n * 8]]
        for o in range(1, 8):
            total += returned[dest[n * 8 + o]]
        sums[n] = total
        return carry

    lax.fori_loop(0, mine * groups, total_of, 0)
    for k in range(1, groups):
        to = (eight + k) & 3
        pltpu.make_async_remote_copy(
            src_ref=sums.at[pl.ds(to * mine, mine)], dst_ref=out.at[eight], send_sem=send_sem.at[1],
            recv_sem=recv_sem.at[1], device_id=(wide, to), device_id_type=MESH,
        ).start()
    kept = pltpu.make_async_copy(sums.at[pl.ds(eight * mine, mine)], out.at[eight], own_sem.at[1])
    kept.start()
    kept.wait()
    three = out.at[pl.ds(0, groups - 1)]
    all_of(three)(recv_sem.at[1]).wait()
    all_of(three)(send_sem.at[1]).wait()
    all_of(others)(send_sem.at[0]).wait()
    for element in range(count):
        pltpu.make_async_copy(made.at[element], galerkin.at[element], out_sem.at[element]).wait()


def finished(where, places, dest, weight, got, rows):
    hoods = dest.shape[0] // 8
    count = weight.shape[0]
    groups = lax.axis_size("eight")
    wides = got.shape[1]
    devices = wides * groups
    smem, vmem = (pl.BlockSpec(memory_space=m) for m in (pltpu.SMEM, pltpu.VMEM))
    f32 = jnp.float32
    return pl.pallas_call(
        finish_kernel,
        in_specs=[smem] * 3 + [vmem] * 3,
        out_specs=[pl.BlockSpec(memory_space=pl.ANY), vmem],
        out_shape=[
            jax.ShapeDtypeStruct((count, 768, 768), f32),
            jax.ShapeDtypeStruct((groups, hoods // groups, SHARE, LANES), f32),
        ],
        scratch_shapes=[
            pltpu.VMEM((count, 768, ECELLS), jnp.bfloat16),
            pltpu.VMEM((count, 768, ECELLS), jnp.bfloat16),
            pltpu.VMEM((count * 8, 48, LANES), f32),
            pltpu.VMEM((wides, groups, SHARE, LANES), f32),
            pltpu.VMEM((count, 768, 768), f32),
            pltpu.VMEM((devices, SHARE, LANES), f32),
            pltpu.VMEM((hoods, SHARE, LANES), f32),
            pltpu.SemaphoreType.DMA((2,)),
            pltpu.SemaphoreType.DMA((2,)),
            pltpu.SemaphoreType.DMA((2,)),
            pltpu.SemaphoreType.DMA((count,)),
        ],
        compiler_params=pltpu.CompilerParams(
            collective_id=1, has_side_effects=True, vmem_limit_bytes=28 * 2**20
        ),
        name="finish",
    )(where, places, dest, weight, got, rows)


def body(start_vectors, conductance, counts, element_of, capacity, coarse_in):
    eight = lax.axis_index("eight")
    me = lax.axis_index("wide") * lax.axis_size("eight") + eight
    hoods = start_vectors.shape[0]
    count = capacity.shape[0]
    dest = (element_of // count).reshape(-1)
    pieces = dest.shape[0]
    names = jnp.arange(pieces, dtype=jnp.int32)
    places = (element_of % count * 8 + jnp.arange(8, dtype=jnp.int32)[None, :]).reshape(-1)
    both = names * 1024 + places
    both = jnp.sum(jnp.where(dest[None, :] == names[:, None], both[None, :], 0), axis=1)
    order, ids = both // 1024, both % 1024
    got, got_rows, table = exchanged(
        order,
        counts,
        start_vectors,
        conductance,
        coarse_in.transpose(0, 2, 1),
        jnp.broadcast_to(ids[None], (8, pieces)),
    )
    wides = table.shape[0]
    came = lax.dynamic_slice_in_dim(table[:, 0], me, 1, axis=1)
    spots = jnp.arange(count * 8, dtype=jnp.int32)[None]
    sources = jnp.arange(wides, dtype=jnp.int32)[:, None]
    where = jnp.sum(jnp.where(came == spots, sources, 0), axis=0)
    galerkin, mine = finished(
        where,
        came[:, 0],
        dest,
        capacity,
        got.reshape(3, wides, 4, ROWS, ECELLS),
        got_rows.reshape(wides, 4, SHARE, LANES),
    )
    galerkin = galerkin * (1.0 / ECELLS)
    mine = mine.transpose(1, 0, 2, 3).reshape(hoods // 4, 48, LANES)
    coarse_out = jnp.concatenate([mine[:, :, :64], mine[:, :, 64:]], axis=1)
    return (galerkin, coarse_out)


def solution(mesh):
    in_specs = (
        P("wide", "eight", None),
        P("wide", None),
        P("wide"),
        P("wide", None),
        P(BOTH, None),
        P(BOTH, None, None),
    )
    out_specs = (P(BOTH, None, None), P(BOTH, None, None))
    return jax.shard_map(body, mesh=mesh, in_specs=in_specs, out_specs=out_specs, check_vma=False)
```

```python
import functools

import jax
import jax.numpy as jnp
from jax import lax
from jax.experimental import pallas as pl
from jax.experimental.pallas import tpu as pltpu
from jax.sharding import PartitionSpec as P

SIDE = 16
PLANE = SIDE * SIDE
CELLS = SIDE * PLANE
ECELLS = 512
ROWS = 8
LANES = 128
SHARE = 12
FRONT = 8
FIELD = FRONT + CELLS + PLANE + 8
GROUP = 4
BOTH = ("wide", "eight")
MESH = pl.DeviceIdType.MESH


def rows_of(a, extra=0, count=SIDE):
    return pl.ds(FRONT + a * PLANE + extra, count)


def clear_ends(field):
    field[pl.ds(0, FRONT)] = jnp.zeros((FRONT, LANES), jnp.float32)
    field[pl.ds(FRONT + CELLS, PLANE + 8)] = jnp.zeros((PLANE + 8, LANES), jnp.float32)


def bring_conductance(cond, field):
    hoods = cond.shape[0]
    clear_ends(field)

    def bring(a, carry):
        plane = cond[:, pl.ds(pl.multiple_of(a * PLANE, PLANE), PLANE)]
        wide = jnp.broadcast_to(plane[:, None, :], (hoods, ROWS, PLANE)).reshape(LANES, PLANE)
        field[rows_of(a, 0, PLANE)] = wide.T
        return carry

    lax.fori_loop(0, SIDE, bring, 0)


def link_weights(coef, field):
    spot = lax.broadcasted_iota(jnp.int32, (SIDE, LANES), 0)
    ends = ((spot == 0) | (spot == SIDE - 1)).astype(jnp.float32)

    def one(a, largest):
        ahead = jnp.where(a < SIDE - 1, 0.5, 0.0)
        behind = jnp.where(a > 0, 0.5, 0.0)
        rim = 2.0 - 2.0 * (ahead + behind)
        last_b = None
        for b in range(SIDE):
            own = field[rows_of(a, b * SIDE)]
            link_a = ahead * (own + field[rows_of(a, b * SIDE + PLANE)])
            past = jnp.maximum(a - 1, 0)
            past_a = behind * (own + field[rows_of(past, b * SIDE)])
            edge = own * (ends + (rim + (1.0 if b in (0, SIDE - 1) else 0.0)))
            next_c = jnp.where(spot < SIDE - 1, 0.5 * (own + field[rows_of(a, b * SIDE + 1)]), 0.0)
            last_c = jnp.where(spot > 0, 0.5 * (own + field[rows_of(a, b * SIDE - 1)]), 0.0)
            edge += next_c + last_c
            diagonal = edge + link_a + past_a
            if b < SIDE - 1:
                link_b = 0.5 * (own + field[rows_of(a, b * SIDE + SIDE)])
                coef[1, pl.ds(a * PLANE + b * SIDE, SIDE)] = link_b
                diagonal += link_b
            if last_b is not None:
                diagonal += last_b
            last_b = link_b
            coef[0, pl.ds(a * PLANE + b * SIDE, SIDE)] = link_a
            coef[2, pl.ds(a * PLANE + b * SIDE, SIDE)] = next_c
            coef[3, pl.ds(a * PLANE + b * SIDE, SIDE)] = last_c
            coef[4, pl.ds(a * PLANE + b * SIDE, SIDE)] = edge
            largest = jnp.maximum(largest, diagonal)
        return largest

    largest = lax.fori_loop(0, SIDE, one, jnp.zeros((SIDE, LANES), jnp.float32))
    radius = 0.4375 * 2.0 * jnp.max(largest, axis=0, keepdims=True)
    scale = jnp.broadcast_to(2.0 / radius, (SIDE, LANES))

    def fit(a, carry):
        for b in range(SIDE):
            at = pl.ds(a * PLANE + b * SIDE, SIDE)
            for k in range(5):
                if k == 1 and b == SIDE - 1:
                    continue
                value = coef[k, at] * scale
                coef[k, at] = value - 18.0 / 7.0 if k == 4 else value
        return carry

    lax.fori_loop(0, SIDE, fit, 0)


def sweep(coef, now, old, flux, first=False, squares=False):
    flux[...] = jnp.zeros_like(flux)

    def one(a, total):
        last_b = None
        here = now[rows_of(a)]
        for base in range(0, SIDE, GROUP):
            results = []
            for b in range(base, base + GROUP):
                at = pl.ds(a * PLANE + b * SIDE, SIDE)
                result = coef[4, at] * here + flux[pl.ds(b * SIDE, SIDE)]
                if last_b is not None:
                    result += last_b
                across = coef[0, at] * (now[rows_of(a, b * SIDE + PLANE)] - here)
                result -= across
                result -= coef[2, at] * now[rows_of(a, b * SIDE + 1)]
                result -= coef[3, at] * now[rows_of(a, b * SIDE - 1)]
                if b < SIDE - 1:
                    ahead = now[rows_of(a, b * SIDE + SIDE)]
                    last_b = coef[1, at] * (ahead - here)
                    result -= last_b
                    here = ahead
                result = 0.5 * result if first else result - old[rows_of(a, b * SIDE)]
                results.append((b, across, result))
            for b, across, result in results:
                flux[pl.ds(b * SIDE, SIDE)] = across
                old[rows_of(a, b * SIDE)] = result
                if squares:
                    total += result * result
        return total

    return lax.fori_loop(0, SIDE, one, jnp.zeros((SIDE, LANES), jnp.float32))


def filtered_chunk(chunk, start, coef, even, odd, flux, meanwhile=None):
    hoods, width = start.shape[:2]
    clear_ends(even)
    clear_ends(odd)

    def bring(a, carry):
        plane = start[:, :, pl.ds(pl.multiple_of(a * PLANE, PLANE), PLANE)].astype(jnp.float32)
        plane = plane[:, chunk * ROWS : (chunk + 1) * ROWS].reshape(LANES, PLANE)
        even[rows_of(a, 0, PLANE)] = plane.T
        return carry

    lax.fori_loop(0, SIDE, bring, 0)
    sweep(coef, even, odd, flux, first=True)
    if meanwhile is not None:
        meanwhile()

    def two(step, carry):
        sweep(coef, odd, even, flux)
        sweep(coef, even, odd, flux)
        return carry

    lax.fori_loop(0, 2, two, 0)
    total = sweep(coef, odd, even, flux, squares=True)
    return jnp.sum(total, axis=0, keepdims=True) * (1.0 / CELLS)


def hat(at):
    return min(at + 0.5, SIDE - 0.5 - at) / (SIDE // 2)


def octant_of(field, scale, octant):
    dx, dy, dz = octant // 4, octant // 2 % 2, octant % 2
    spot = lax.broadcasted_iota(jnp.int32, (8, LANES), 0).astype(jnp.float32) + 8.0 * dz
    scale = scale * (jnp.minimum(spot + 0.5, SIDE - 0.5 - spot) * (2.0 / SIDE))
    parts = []
    for a in range(8 * dx, 8 * dx + 8):
        for b in range(8 * dy, 8 * dy + 8):
            cells = field[pl.ds(FRONT + a * PLANE + b * SIDE + 8 * dz, 8)]
            parts.append(cells * (scale * (hat(a) * hat(b))))
    return jnp.concatenate(parts, axis=0).T


def partner(k, wide, eight):
    z, x, core, four = wide >> 3, wide >> 1, wide, k >> 2
    z = (z + (k >> 4) + 2 * four + 3 * k) & 3
    x = (x + four + k) & 3
    core = (core + (k >> 6) + k) & 1
    return (z * 4 + x) * 2 + core, (eight + k) & 3


def greet(wide, eight):
    barrier = pltpu.get_barrier_semaphore()
    groups, wides = lax.axis_size("eight"), lax.axis_size("wide")

    def tell(to_wide, to_eight):
        pl.semaphore_signal(barrier, inc=1, device_id=(to_wide, to_eight), device_id_type=MESH)

    def one(k, carry):
        to_wide = (wide + k) & 31
        for to_eight in range(groups):
            tell(to_wide, to_eight)
        return carry

    lax.fori_loop(1, wides, one, 0)
    for k in range(1, groups):
        tell(wide, (eight + k) & 3)
    return lambda: pl.semaphore_wait(barrier, groups * wides - 1)


def all_of(ref):
    return lambda sem: pltpu.make_async_copy(ref, ref, sem)


def exchange_kernel(
    order, counts, start, cond_hbm, coarse_hbm, ids,
    got, got_rows, table,
    coef, even, odd, flux, pieces, outgoing, coarse_rows, outgoing_rows, cond, coarse,
    send_sem, recv_sem, own_sem,
):
    wide, eight = lax.axis_index("wide"), lax.axis_index("eight")
    groups, wides = lax.axis_size("eight"), lax.axis_size("wide")
    devices = groups * wides
    me = wide * groups + eight
    hoods = start.shape[0]
    mine = coarse.shape[0]

    bring_cond = pltpu.make_async_copy(cond_hbm, cond, own_sem.at[6])
    bring_coarse = pltpu.make_async_copy(coarse_hbm, coarse, own_sem.at[7])
    bring_cond.start()
    bring_coarse.start()
    all_here = greet(wide, eight)
    lane = lax.broadcasted_iota(jnp.int32, (8, LANES), 1)
    limit = jnp.zeros((8, LANES), jnp.int32)
    for n in range(hoods):
        limit = jnp.where(lane // ROWS == n, counts[n], limit)
    limit -= eight * 24 + lane % ROWS
    bring_cond.wait()
    bring_coarse.wait()
    bring_conductance(cond, even)
    link_weights(coef, even)
    for n in range(mine):
        turned = coarse[n].T
        packed = jnp.concatenate([turned[:48], turned[48:]], axis=1)
        coarse_rows[pl.ds(eight * mine + n, 1)] = packed[None]
    all_here()
    own_rows = coarse_rows.at[pl.ds(eight * mine, mine)]
    for k in range(1, groups):
        pltpu.make_async_remote_copy(
            src_ref=own_rows, dst_ref=own_rows, send_sem=send_sem.at[3], recv_sem=recv_sem.at[3],
            device_id=(wide, (eight + k) % groups), device_id_type=MESH,
        ).start()

    def tell(k, carry):
        pltpu.make_async_remote_copy(
            src_ref=ids, dst_ref=table.at[wide], send_sem=send_sem.at[4], recv_sem=recv_sem.at[4],
            device_id=((wide + k) % wides, eight), device_id_type=MESH,
        ).start()
        return carry

    lax.fori_loop(1, wides, tell, 0)
    own_ids = pltpu.make_async_copy(ids, table.at[wide], own_sem.at[4])
    own_ids.start()

    three = coarse_rows.at[pl.ds(0, mine * (groups - 1))]
    first = eight * SHARE

    def take_rows(to):
        outgoing_rows[pl.ds(to, 1)] = coarse_rows[pl.ds(order[to] // 8, 1), pl.ds(first, SHARE)]

    def send_rows(k, carry):
        to_wide, to_eight = partner(k, wide, eight)
        to = to_wide * groups + to_eight
        take_rows(to)
        pltpu.make_async_remote_copy(
            src_ref=outgoing_rows.at[to], dst_ref=got_rows.at[me], send_sem=send_sem.at[5],
            recv_sem=recv_sem.at[5], device_id=(to_wide, to_eight), device_id_type=MESH,
        ).start()
        return carry

    kept_rows = pltpu.make_async_copy(outgoing_rows.at[me], got_rows.at[me], own_sem.at[5])

    def send_all_rows():
        all_of(three)(recv_sem.at[3]).wait()
        lax.fori_loop(1, devices, send_rows, 0)
        take_rows(me)
        kept_rows.start()

    kept = []
    for chunk in range(3):
        mean = filtered_chunk(
            chunk, start, coef, even, odd, flux, send_all_rows if chunk == 0 else None
        )
        live = (limit > chunk * ROWS).astype(jnp.float32)
        scale = jnp.broadcast_to(lax.rsqrt(mean + 1e-05), (8, LANES)) * live
        for octant in range(8):
            turned = octant_of(even, scale, octant)
            for n in range(hoods):
                pieces[n * 8 + octant] = turned[n * ROWS : (n + 1) * ROWS]

        def send(k, carry):
            to_wide, to_eight = partner(k, wide, eight)
            to = to_wide * groups + to_eight
            outgoing[chunk, pl.ds(to, 1)] = pieces[pl.ds(order[to], 1)]
            pltpu.make_async_remote_copy(
                src_ref=outgoing.at[chunk, to], dst_ref=got.at[chunk, me], send_sem=send_sem.at[chunk],
                recv_sem=recv_sem.at[chunk], device_id=(to_wide, to_eight), device_id_type=MESH,
            ).start()
            return carry

        lax.fori_loop(1, devices, send, 0)
        outgoing[chunk, pl.ds(me, 1)] = pieces[pl.ds(order[me], 1)]
        kept.append(pltpu.make_async_copy(outgoing.at[chunk, me], got.at[chunk, me], own_sem.at[chunk]))
        kept[-1].start()

    own_ids.wait()
    kept_rows.wait()
    all_of(three)(send_sem.at[3]).wait()
    others = table.at[pl.ds(0, wides - 1)]
    all_of(others)(send_sem.at[4]).wait()
    all_of(others)(recv_sem.at[4]).wait()
    others = got_rows.at[pl.ds(0, devices - 1)]
    all_of(others)(send_sem.at[5]).wait()
    all_of(others)(recv_sem.at[5]).wait()
    for chunk in range(3):
        kept[chunk].wait()
        others = got.at[chunk, pl.ds(0, devices - 1)]
        all_of(others)(send_sem.at[chunk]).wait()
        all_of(others)(recv_sem.at[chunk]).wait()


def exchanged(order, counts, start, cond, coarse, ids):
    hoods = start.shape[0]
    pieces = hoods * 8
    wides = lax.axis_size("wide")
    vmem = pl.BlockSpec(memory_space=pltpu.VMEM)
    hbm = pl.BlockSpec(memory_space=pl.ANY)
    f32 = jnp.float32
    return pl.pallas_call(
        exchange_kernel,
        in_specs=[pl.BlockSpec(memory_space=pltpu.SMEM)] * 2 + [vmem, hbm, hbm, vmem],
        out_specs=[hbm] * 3,
        out_shape=[
            jax.ShapeDtypeStruct((3, pieces, ROWS, ECELLS), f32),
            jax.ShapeDtypeStruct((pieces, SHARE, LANES), f32),
            jax.ShapeDtypeStruct((wides,) + ids.shape, jnp.int32),
        ],
        scratch_shapes=[
            pltpu.VMEM((5, CELLS, LANES), f32),
            pltpu.VMEM((FIELD, LANES), f32),
            pltpu.VMEM((FIELD, LANES), f32),
            pltpu.VMEM((PLANE, LANES), f32),
            pltpu.VMEM((pieces, ROWS, ECELLS), f32),
            pltpu.VMEM((3, pieces, ROWS, ECELLS), f32),
            pltpu.VMEM((hoods, 48, LANES), f32),
            pltpu.VMEM((pieces, SHARE, LANES), f32),
            pltpu.VMEM(cond.shape, f32),
            pltpu.VMEM(coarse.shape, f32),
            pltpu.SemaphoreType.DMA((6,)),
            pltpu.SemaphoreType.DMA((6,)),
            pltpu.SemaphoreType.DMA((8,)),
        ],
        compiler_params=pltpu.CompilerParams(
            collective_id=0, has_side_effects=True, vmem_limit_bytes=36 * 2**20),
        name="exchange",
    )(order, counts, start, cond, coarse, ids)


def split(wide_value):
    high = wide_value.astype(jnp.bfloat16)
    return high, (wide_value - high.astype(jnp.float32)).astype(jnp.bfloat16)


def thrice(left, right, dims):
    dot = functools.partial(
        lax.dot_general, dimension_numbers=(dims, ((), ())), preferred_element_type=jnp.float32
    )
    (lh, ll), (rh, rl) = left, right
    return dot(lh, rh) + (dot(lh, rl) + dot(ll, rh))


def finish_kernel(
    where, places, dest, weight, pieces, rows,
    galerkin, out,
    high, low, applied, back, made, returned, sums, send_sem, recv_sem, own_sem, out_sem,
):
    wide, eight = lax.axis_index("wide"), lax.axis_index("eight")
    groups, wides = lax.axis_size("eight"), lax.axis_size("wide")
    devices = groups * wides
    me = wide * groups + eight
    mine = out.shape[1]
    count = weight.shape[0]
    all_here = greet(wide, eight)

    def apply(element, carry):
        root = jnp.sqrt(weight[pl.ds(element, 1)])
        vecs = []
        for o in range(8):
            source = where[element * 8 + o]
            parts = [pieces[ch, source, g] for g in range(4) for ch in range(3)]
            whole = jnp.concatenate(parts, axis=0) * root
            high[element, pl.ds(o * 96, 96)], low[element, pl.ds(o * 96, 96)] = split(whole)
            packed = jnp.concatenate([rows[source, g] for g in range(4)], axis=0)
            vecs += [packed[:, :64], packed[:, 64:]]
        vec = jnp.concatenate(vecs, axis=0).T
        whole = (high[element], low[element])
        seen = thrice(split(vec), whole, ((1,), (0,)))
        product = thrice(whole, split(seen * (1.0 / ECELLS)), ((1,), (1,)))
        for o in range(8):
            halves = [product[o * 96 + h * 48 : o * 96 + h * 48 + 48] for h in range(2)]
            applied[element * 8 + o] = jnp.concatenate(halves, axis=1)
        return carry

    lax.fori_loop(0, count, apply, 0)

    def place(source, carry):
        packed = applied[places[source]]
        for g in range(4):
            back[source, g] = packed[g * SHARE : (g + 1) * SHARE]
        return carry

    lax.fori_loop(0, wides, place, 0)
    all_here()

    def send(k, carry):
        to_wide, to_eight = partner(k, wide, eight)
        pltpu.make_async_remote_copy(
            src_ref=back.at[to_wide, to_eight], dst_ref=returned.at[me], send_sem=send_sem.at[0],
            recv_sem=recv_sem.at[0], device_id=(to_wide, to_eight), device_id_type=MESH,
        ).start()
        return carry

    lax.fori_loop(1, devices, send, 0)
    kept = pltpu.make_async_copy(back.at[wide, eight], returned.at[me], own_sem.at[0])
    kept.start()

    def matrix(element, carry):
        def block(i):
            return element, pl.ds(i * 256, 256)

        for i in range(3):
            for j in range(i, 3):
                product = thrice(
                    (high[block(i)], low[block(i)]), (high[block(j)], low[block(j)]), ((1,), (1,))
                )
                made[element, pl.ds(i * 256, 256), pl.ds(j * 256, 256)] = product
                if i != j:
                    made[element, pl.ds(j * 256, 256), pl.ds(i * 256, 256)] = product.T
        pltpu.make_async_copy(made.at[element], galerkin.at[element], out_sem.at[element]).start()
        return carry

    lax.fori_loop(0, count, matrix, 0)
    kept.wait()
    others = returned.at[pl.ds(0, devices - 1)]
    all_of(others)(recv_sem.at[0]).wait()

    def total_of(n, carry):
        total = returned[dest[n * 8]]
        for o in range(1, 8):
            total += returned[dest[n * 8 + o]]
        sums[n] = total
        return carry

    lax.fori_loop(0, mine * groups, total_of, 0)
    for k in range(1, groups):
        to = (eight + k) & 3
        pltpu.make_async_remote_copy(
            src_ref=sums.at[pl.ds(to * mine, mine)], dst_ref=out.at[eight], send_sem=send_sem.at[1],
            recv_sem=recv_sem.at[1], device_id=(wide, to), device_id_type=MESH,
        ).start()
    kept = pltpu.make_async_copy(sums.at[pl.ds(eight * mine, mine)], out.at[eight], own_sem.at[1])
    kept.start()
    kept.wait()
    three = out.at[pl.ds(0, groups - 1)]
    all_of(three)(recv_sem.at[1]).wait()
    all_of(three)(send_sem.at[1]).wait()
    all_of(others)(send_sem.at[0]).wait()
    for element in range(count):
        pltpu.make_async_copy(made.at[element], galerkin.at[element], out_sem.at[element]).wait()


def finished(where, places, dest, weight, got, rows):
    hoods = dest.shape[0] // 8
    count = weight.shape[0]
    groups = lax.axis_size("eight")
    wides = got.shape[1]
    devices = wides * groups
    smem, vmem = (pl.BlockSpec(memory_space=m) for m in (pltpu.SMEM, pltpu.VMEM))
    f32 = jnp.float32
    return pl.pallas_call(
        finish_kernel,
        in_specs=[smem] * 3 + [vmem] * 3,
        out_specs=[pl.BlockSpec(memory_space=pl.ANY), vmem],
        out_shape=[
            jax.ShapeDtypeStruct((count, 768, 768), f32),
            jax.ShapeDtypeStruct((groups, hoods // groups, SHARE, LANES), f32),
        ],
        scratch_shapes=[
            pltpu.VMEM((count, 768, ECELLS), jnp.bfloat16),
            pltpu.VMEM((count, 768, ECELLS), jnp.bfloat16),
            pltpu.VMEM((count * 8, 48, LANES), f32),
            pltpu.VMEM((wides, groups, SHARE, LANES), f32),
            pltpu.VMEM((count, 768, 768), f32),
            pltpu.VMEM((devices, SHARE, LANES), f32),
            pltpu.VMEM((hoods, SHARE, LANES), f32),
            pltpu.SemaphoreType.DMA((2,)),
            pltpu.SemaphoreType.DMA((2,)),
            pltpu.SemaphoreType.DMA((2,)),
            pltpu.SemaphoreType.DMA((count,)),
        ],
        compiler_params=pltpu.CompilerParams(
            collective_id=1, has_side_effects=True, vmem_limit_bytes=28 * 2**20
        ),
        name="finish",
    )(where, places, dest, weight, got, rows)


def body(start_vectors, conductance, counts, element_of, capacity, coarse_in):
    eight = lax.axis_index("eight")
    me = lax.axis_index("wide") * lax.axis_size("eight") + eight
    hoods = start_vectors.shape[0]
    count = capacity.shape[0]
    dest = (element_of // count).reshape(-1)
    pieces = dest.shape[0]
    names = jnp.arange(pieces, dtype=jnp.int32)
    places = (element_of % count * 8 + jnp.arange(8, dtype=jnp.int32)[None, :]).reshape(-1)
    both = names * 1024 + places
    both = jnp.sum(jnp.where(dest[None, :] == names[:, None], both[None, :], 0), axis=1)
    order, ids = both // 1024, both % 1024
    got, got_rows, table = exchanged(
        order,
        counts,
        start_vectors,
        conductance,
        coarse_in.transpose(0, 2, 1),
        jnp.broadcast_to(ids[None], (8, pieces)),
    )
    wides = table.shape[0]
    came = lax.dynamic_slice_in_dim(table[:, 0], me, 1, axis=1)
    spots = jnp.arange(count * 8, dtype=jnp.int32)[None]
    sources = jnp.arange(wides, dtype=jnp.int32)[:, None]
    where = jnp.sum(jnp.where(came == spots, sources, 0), axis=0)
    galerkin, mine = finished(
        where,
        came[:, 0],
        dest,
        capacity,
        got.reshape(3, wides, 4, ROWS, ECELLS),
        got_rows.reshape(wides, 4, SHARE, LANES),
    )
    galerkin = galerkin * (1.0 / ECELLS)
    mine = mine.transpose(1, 0, 2, 3).reshape(hoods // 4, 48, LANES)
    coarse_out = jnp.concatenate([mine[:, :, :64], mine[:, :, 64:]], axis=1)
    return (galerkin, coarse_out)


def solution(mesh):
    in_specs = (
        P("wide", "eight", None),
        P("wide", None),
        P("wide"),
        P("wide", None),
        P(BOTH, None),
        P(BOTH, None, None),
    )
    out_specs = (P(BOTH, None, None), P(BOTH, None, None))
    return jax.shard_map(body, mesh=mesh, in_specs=in_specs, out_specs=out_specs, check_vma=False)
```
